256 devices in a mesh: tm: 128 (over z, x_lo, y, core), head: 2 (over x_hi).
Axes of the slice: x: 4 (x_hi: 2, x_lo: 2; x = x_hi * 2 + x_lo), y: 4, z: 8, core: 2. Of those that a mesh axis runs over, the one named last changes fastest.
Arguments:
- queries: bfloat16 [65536, 1024], P('tm', 'head'), may hold values from -16 to 16
- keys: bfloat16 [65536, 1024], P('tm', 'head'), may hold values from -16 to 16
- values: bfloat16 [65536, 1024], P('tm', 'head'), may hold values from -6 to 6
- grad_attn: bfloat16 [65536, 1024], P('tm', 'head'), may hold values from -128 to 128
- w_query: bfloat16 [1024, 1024], P(None, 'head'), may hold values from -0.1875 to 0.1875
- w_key: bfloat16 [1024, 1024], P(None, 'head'), may hold values from -0.1875 to 0.1875
- w_value: bfloat16 [1024, 1024], P(None, 'head'), may hold values from -0.1875 to 0.1875
Outputs:
- grad_frames: bfloat16 [65536, 1024], P(('tm', 'head'))
The draws below stay inside these ranges and needn't reach their ends.
All inputs are finite; a program needn't handle non-finite values.
Results may differ from the reference program's by a relative error of at most 0.015.
Values may be sent and summed in bfloat16 or wider, within the bound.
No kernel may reach another device: no remote copies, remote signals or barrier semaphores. Data moves between devices by JAX's collectives and lax.ppermute only.
A program may use at most 128 MiB of HBM per device.

```python
import jax
import jax.numpy as jnp
from jax import lax

HEADS = 16
HEAD_DIM = 64
SEGMENT_FRAMES = 512
D = 1024
FRAMES = 65536
DILATION_ONE = 4
DILATION_TWO = 16
DILATION_THREE = 64


def draw_queries(key, part):
    key = jax.random.fold_in(key, 11)
    base = jnp.clip(jax.random.normal(key, (FRAMES, D), jnp.float32), -4.0, 4.0)
    return base.astype(jnp.bfloat16)


def draw_keys(key, part):
    key = jax.random.fold_in(key, 23)
    base = jnp.clip(jax.random.normal(key, (FRAMES, D), jnp.float32), -4.0, 4.0)
    return base.astype(jnp.bfloat16)


def block_scale(rng, shape, cuts, low, largest):
    def one(dim, blocks):
        draws = jax.random.uniform(jax.random.fold_in(jax.random.fold_in(rng, 6), dim), (blocks,), jnp.float32, low / len(cuts), largest / len(cuts))
        return jnp.repeat(jnp.exp(draws), shape[dim] // blocks).reshape((-1,) + (1,) * (len(shape) - dim - 1))

    gain = one(*cuts[0])
    for cut in cuts[1:]:
        gain = gain * one(*cut)
    return gain


def centred(own_key, dims, width, most, shards=(), held_as=jnp.bfloat16):
    values = width * jax.random.normal(own_key, dims, jnp.float32)
    if shards:
        values = values * block_scale(own_key, dims, shards, -0.22, 0.18)
    return jnp.clip(values, -most, most).astype(held_as)


def setup_inputs(seed: int = 0) -> dict:
    key_list = jax.random.split(jax.random.key(seed), 8)
    queries = draw_queries(jax.random.fold_in(key_list[7], 71), 0)
    keys = draw_keys(jax.random.fold_in(key_list[7], 71), 0)
    values = centred(key_list[2], (FRAMES, D), 1.0, 6.0, ((0, 128), (1, 2)))
    grad_attn = centred(key_list[3], (FRAMES, D), 24.0, 128.0, ((0, 128), (1, 2)))
    w_query = centred(key_list[4], (D, D), D ** -0.5, 0.1875, ((1, 2),))
    w_key = centred(key_list[5], (D, D), D ** -0.5, 0.1875, ((1, 2),))
    w_value = centred(key_list[6], (D, D), D ** -0.5, 0.1875, ((1, 2),))
    return dict(queries=queries, keys=keys, values=values, grad_attn=grad_attn, w_query=w_query, w_key=w_key, w_value=w_value)


def round_keep(array):
    return lax.optimization_barrier(array.astype(jnp.bfloat16)).astype(jnp.float32)


def branch_rows(array, dilation):
    picked = array[::dilation]
    return picked.reshape(-1, SEGMENT_FRAMES, HEADS, HEAD_DIM)


def segment_forward(query, key_block, value_block):
    score_scale = HEAD_DIM ** -0.5
    query_f = query.astype(jnp.float32)
    key_f = key_block.astype(jnp.float32)
    value_f = value_block.astype(jnp.float32)
    scores = jnp.einsum("qhd,khd->hqk", query_f, key_f) * score_scale
    highest = jnp.max(scores, axis=2)
    shifted = jnp.exp(scores - highest[:, :, None])
    totals = jnp.sum(shifted, axis=2)
    weighted = jnp.einsum("hqk,khd->hqd", round_keep(shifted), value_f)
    return highest, totals, weighted


def segment_backward(query, key_block, value_block, grad_rows, lse_rows, delta_rows):
    score_scale = HEAD_DIM ** -0.5
    query_f = query.astype(jnp.float32)
    key_f = key_block.astype(jnp.float32)
    value_f = value_block.astype(jnp.float32)
    grad_f = grad_rows.astype(jnp.float32)
    scores = jnp.einsum("qhd,khd->hqk", query_f, key_f) * score_scale
    probs = jnp.exp(scores - jnp.transpose(lse_rows)[:, :, None])
    grad_value = jnp.einsum("hqk,qhd->khd", round_keep(probs), grad_f)
    grad_prob = jnp.einsum("qhd,khd->hqk", grad_f, value_f)
    grad_score = round_keep(probs * (grad_prob - jnp.transpose(delta_rows)[:, :, None]))
    grad_query = jnp.einsum("hqk,khd->qhd", grad_score, key_f) * score_scale
    grad_key = jnp.einsum("hqk,qhd->khd", grad_score, query_f) * score_scale
    return grad_query, grad_key, grad_value


def reference(queries, keys, values, grad_attn, w_query, w_key, w_value):
    dilation_steps = [1, DILATION_ONE, DILATION_TWO, DILATION_THREE]
    grad_heads = grad_attn.reshape(FRAMES, HEADS, HEAD_DIM)
    highest = None
    totals = None
    weighted = None
    for position, dilation in enumerate(dilation_steps):
        operands = (branch_rows(queries, dilation), branch_rows(keys, dilation), branch_rows(values, dilation))
        top_seg, sum_seg, acc_seg = lax.map(lambda bundle: segment_forward(bundle[0], bundle[1], bundle[2]), operands)
        top_rows = jnp.transpose(top_seg, (0, 2, 1)).reshape(-1, HEADS)
        sum_rows = jnp.transpose(sum_seg, (0, 2, 1)).reshape(-1, HEADS)
        acc_rows = jnp.transpose(acc_seg, (0, 2, 1, 3)).reshape(-1, HEADS, HEAD_DIM)
        if position == 0:
            highest, totals, weighted = top_rows, sum_rows, acc_rows
        else:
            old_top = highest[::dilation]
            new_top = jnp.maximum(old_top, top_rows)
            keep_old = jnp.exp(old_top - new_top)
            take_new = jnp.exp(top_rows - new_top)
            totals = totals.at[::dilation].set(totals[::dilation] * keep_old + sum_rows * take_new)
            weighted = weighted.at[::dilation].set(weighted[::dilation] * keep_old[:, :, None] + acc_rows * take_new[:, :, None])
            highest = highest.at[::dilation].set(new_top)
    lse_all = highest + jnp.log(totals)
    attn = weighted / totals[:, :, None]
    delta = jnp.sum(attn * grad_heads.astype(jnp.float32), axis=2)
    grad_q = jnp.zeros((FRAMES, HEADS, HEAD_DIM), jnp.float32)
    grad_k = jnp.zeros((FRAMES, HEADS, HEAD_DIM), jnp.float32)
    grad_v = jnp.zeros((FRAMES, HEADS, HEAD_DIM), jnp.float32)
    for dilation in dilation_steps:
        operands = (branch_rows(queries, dilation), branch_rows(keys, dilation), branch_rows(values, dilation),
                    grad_heads[::dilation].reshape(-1, SEGMENT_FRAMES, HEADS, HEAD_DIM),
                    lse_all[::dilation].reshape(-1, SEGMENT_FRAMES, HEADS), delta[::dilation].reshape(-1, SEGMENT_FRAMES, HEADS))
        part_q, part_k, part_v = lax.map(lambda bundle: segment_backward(*bundle), operands)
        grad_q = grad_q.at[::dilation].add(part_q.reshape(-1, HEADS, HEAD_DIM))
        grad_k = grad_k.at[::dilation].add(part_k.reshape(-1, HEADS, HEAD_DIM))
        grad_v = grad_v.at[::dilation].add(part_v.reshape(-1, HEADS, HEAD_DIM))
    round_q = grad_q.reshape(FRAMES, D).astype(jnp.bfloat16)
    round_k = grad_k.reshape(FRAMES, D).astype(jnp.bfloat16)
    round_v = grad_v.reshape(FRAMES, D).astype(jnp.bfloat16)
    summed = jnp.dot(round_q, w_query.T, preferred_element_type=jnp.float32)
    summed = summed + jnp.dot(round_k, w_key.T, preferred_element_type=jnp.float32)
    summed = summed + jnp.dot(round_v, w_value.T, preferred_element_type=jnp.float32)
    return summed.astype(jnp.bfloat16)
```

```python
import functools

import jax
import jax.numpy as jnp
import numpy as np
from jax import lax
from jax.experimental import pallas as pl
from jax.experimental.pallas import tpu as pltpu
from jax.sharding import PartitionSpec as P

BF16 = jnp.bfloat16
F32 = jnp.float32
ROWS = 512
DIL = 128
REST = ROWS - DIL
LANES = 128
HEADS = 8
STAT_ROWS = 16
VMEM = 48 * 1024 * 1024
LOW = -1e30


def frame_order():
    r = np.arange(DIL)
    dil = np.concatenate([r[r % 16 == 0], r[(r % 4 == 0) & (r % 16 != 0)], r[r % 4 != 0]])
    f = np.arange(ROWS)
    return dil, np.concatenate([dil * 4, f[f % 4 != 0]])


def one_hot(index, width):
    out = np.zeros((len(index), width), np.float32)
    out[np.arange(len(index)), index] = 1
    return out


def dot_tt(a, b):
    return lax.dot_general(a, b, (((1,), (1,)), ((), ())), preferred_element_type=F32)


def dot(a, b):
    return jnp.dot(a, b, preferred_element_type=F32)


def half_mask(side):
    lane = lax.broadcasted_iota(jnp.int32, (1, LANES), 1)
    return jnp.where((lane >= 64) == (side == 1), 1.0, 0.0)


def choose(first, second):
    lane = lax.broadcasted_iota(jnp.int32, first.shape, 1)
    return jnp.where(lane < 64, first, second)


def stats(scores, grad_prob):
    top = jnp.max(scores, axis=0, keepdims=True)
    e = jnp.exp(scores - top)
    total = jnp.sum(e, axis=0, keepdims=True)
    delta = jnp.sum(e * grad_prob, axis=0, keepdims=True) / total
    return e, total, top + jnp.log(total), delta


def thirds(x):
    a = x.astype(BF16).astype(F32)
    b = (x - a).astype(BF16).astype(F32)
    return [a, b, x - a - b]


def pack_kernel(perm_ref, q_ref, k_ref, v_ref, g_ref, qo, ko, vo, go, x_ref):
    block = jnp.concatenate([q_ref[...] * BF16(0.125), k_ref[...], v_ref[...], g_ref[...]], axis=1)
    block = dot(perm_ref[...], block).astype(BF16)
    q, k, v, g = (block[:, i * LANES : (i + 1) * LANES] for i in range(4))
    qo[...] = q
    ko[...] = k
    vo[...] = v
    go[...] = g
    for h in range(2):
        mask = half_mask(h).astype(BF16)
        scores = dot_tt(k * mask, q[:DIL])
        grad_prob = dot_tt(v * mask, g[:DIL])
        _, _, lse, delta = stats(scores, grad_prob)
        rows = jnp.concatenate(thirds(lse) + thirds(delta) + [jnp.zeros((STAT_ROWS - 6, LANES), F32)], axis=0)
        cols = slice(h * 64, h * 64 + 64)
        x_ref[h, :DIL, :] = jnp.concatenate([k[:DIL, cols], v[:DIL, cols], q[:DIL, cols], g[:DIL, cols]], axis=1)
        x_ref[h, DIL:, :] = jnp.concatenate([rows, jnp.zeros_like(rows)], axis=1).astype(BF16)


def local_kernel(q_ref, k_ref, v_ref, g_ref, dq_ref, dk_ref, dv_ref):
    q, g = q_ref[DIL:, :], g_ref[DIL:, :]
    k, v = k_ref[...], v_ref[...]
    dq, dk, dv = None, [], []
    for h in range(2):
        mask = half_mask(h).astype(BF16)
        km = k * mask
        scores = dot_tt(km, q)
        grad_prob = dot_tt(v * mask, g)
        e, total, _, delta = stats(scores, grad_prob)
        p = e * (1.0 / total)
        ds = (p * (grad_prob - delta)).astype(BF16)
        dv.append(dot(p.astype(BF16), g))
        dk.append(dot(ds, q))
        part = dot((km * BF16(0.125)).T, ds)
        dq = part if dq is None else dq + part
    dk_ref[...] = choose(*dk)
    dv_ref[...] = choose(*dv)
    dq_ref[...] = dq.T.astype(BF16)


def head_kernel(x_ref, p16_ref, c64_ref, own_ref, dq_ref, part16_ref, part64_ref, stat_ref):
    first = half_mask(0).astype(BF16)
    second = half_mask(1).astype(BF16)

    def products(kv, qg):
        return dot_tt(kv * first, qg), dot_tt(kv * second, qg)

    def grads(kv, qg, scores, grad_prob, lse, delta):
        p = jnp.exp(scores - lse)
        ds = (p * (grad_prob - delta)).astype(BF16)
        dkv = choose(dot(ds, qg), dot(p.astype(BF16), qg))
        dq = dot((kv * (first * BF16(0.125))).T, ds).T
        return dkv, dq

    def spread(row, width, fill):
        lines = []
        for s in range(HEADS):
            piece = row[:, s * width : (s + 1) * width]
            if width < DIL:
                piece = jnp.concatenate([piece, jnp.full((1, DIL - width), fill, F32)], axis=1)
            lines.append(piece)
        return jnp.concatenate(lines, axis=0)

    def collect(table, width):
        return jnp.concatenate([table[s : s + 1, :width] for s in range(HEADS)], axis=1)

    segments = []
    for s in range(2):
        block = x_ref[4 * s : 4 * s + 4, :DIL, :].reshape(4 * DIL, 2 * LANES)
        segments.append((block[:, :LANES], block[:, LANES:]))
    block16 = x_ref[:, :32, :].reshape(256, 2 * LANES)
    kv16 = jnp.concatenate([block16[:, :LANES], p16_ref[...]], axis=0)
    qg16 = block16[:, LANES:]
    qg64 = x_ref[:, :16, LANES:].astype(F32)[:, :8, :].reshape(64, LANES).astype(BF16)
    kv64 = c64_ref[...].reshape(512, LANES)

    lse1, delta1 = [], []
    for s in range(HEADS):
        rows = x_ref[s, DIL:, :LANES].astype(F32)
        lse1.append(rows[0:1] + rows[1:2] + rows[2:3])
        delta1.append(rows[3:4] + rows[4:5] + rows[5:6])
    lses = [jnp.concatenate(lse1, axis=0)]
    deltas = [jnp.concatenate(delta1, axis=0)]

    made = [products(kv, qg) for kv, qg in segments]
    got = [stats(*pair) for pair in made]
    lses.append(spread(jnp.concatenate([got[0][2], got[1][2]], axis=1), DIL, LOW))
    deltas.append(spread(jnp.concatenate([got[0][3], got[1][3]], axis=1), DIL, 0.0))
    made16 = products(kv16, qg16)
    got = stats(*made16)
    lses.append(spread(got[2], 32, LOW))
    deltas.append(spread(got[3], 32, 0.0))
    made64 = products(kv64, qg64)
    got = stats(*made64)
    lses.append(spread(got[2], 8, LOW))
    deltas.append(spread(got[3], 8, 0.0))

    top = functools.reduce(jnp.maximum, lses)
    parts = [jnp.exp(x - top) for x in lses]
    total = sum(parts)
    lse = top + jnp.log(total)
    delta = sum(w * d for w, d in zip(parts, deltas)) / total
    stat_ref[0] = lse
    stat_ref[1] = delta

    for s in range(2):
        row = [jnp.concatenate([t[4 * s + i : 4 * s + i + 1] for i in range(4)], axis=1) for t in (lse, delta)]
        dkv, dq = grads(*segments[s], *made[s], *row)
        own_ref[4 * s : 4 * s + 4] = dkv.reshape(4, DIL, LANES)
        dq_ref[4 * s : 4 * s + 4] = dq.reshape(4, DIL, LANES)
    dkv, dq = grads(kv16, qg16, *made16, collect(lse, 32), collect(delta, 32))
    own_ref[:, :32, :] = own_ref[:, :32, :] + dkv[:256].reshape(HEADS, 32, LANES)
    part16_ref[...] = dkv[256:].astype(BF16)
    dq_ref[:, :32, :] = dq_ref[:, :32, :] + dq.reshape(HEADS, 32, LANES)
    dkv, dq = grads(kv64, qg64, *made64, collect(lse, 8), collect(delta, 8))
    part64_ref[...] = dkv.reshape(HEADS, 64, LANES).astype(BF16)
    dq_ref[:, :8, :] = dq_ref[:, :8, :] + dq.reshape(HEADS, 8, LANES)


def gather_kernel(own_ref, dq_ref, got16_ref, got64_ref, out_ref):
    got16 = got16_ref[...].astype(F32).reshape(HEADS, 32, LANES)
    got64 = got64_ref[...].astype(F32)
    got64 = sum(got64[i] for i in range(HEADS)).reshape(HEADS, 8, LANES)
    first = got16[:, :8] + got64
    dkv = own_ref[...]
    dkv = jnp.concatenate([dkv[:, :8] + first, dkv[:, 8:32] + got16[:, 8:], dkv[:, 32:]], axis=1)
    out_ref[:, :DIL, :] = dkv.astype(BF16)
    for s in range(HEADS):
        dq = dq_ref[s]
        out_ref[s, DIL:, :] = jnp.concatenate([dq[:64, :64], dq[64:, :64]], axis=1).astype(BF16)


def rest_kernel(
    place_ref, q_ref, k_ref, v_ref, g_ref, dq1_ref, dk1_ref, dv1_ref, st_ref, wq_ref, wk_ref, wv_ref,
    dil_ref, keep_ref, send_ref, dq_s, dk_s, dv_s, out_s,
):
    slab = pl.program_id(0)
    line = place_ref[0]
    head = place_ref[1]
    q, g = q_ref[:DIL, :], g_ref[:DIL, :]
    k, v = k_ref[...], v_ref[...]
    dq, dk, dv = None, [], []
    for h in range(2):
        mask = half_mask(h).astype(BF16)
        km = k * mask
        scores = dot_tt(km, q)
        grad_prob = dot_tt(v * mask, g)
        at = jnp.bitwise_xor(2 * slab + h, line)
        lse = st_ref[at, 0, pl.ds(line, 1), :]
        delta = st_ref[at, 1, pl.ds(line, 1), :]
        p = jnp.exp(scores - lse)
        ds = (p * (grad_prob - delta)).astype(BF16)
        dv.append(dot(p.astype(BF16), g))
        dk.append(dot(ds, q))
        part = dot((km * BF16(0.125)).T, ds)
        dq = part if dq is None else dq + part
    dk = choose(*dk) + dk1_ref[...]
    dv = choose(*dv) + dv1_ref[...]
    dil_ref[0] = dq.T
    dil_ref[1] = dk[:DIL]
    dil_ref[2] = dv[:DIL]
    for s in range(4):

        @pl.when(slab == s)
        def _():
            cols = slice(s * LANES, (s + 1) * LANES)
            dq_s[:, cols] = dq1_ref[...]
            dk_s[:, cols] = dk[DIL:].astype(BF16)
            dv_s[:, cols] = dv[DIL:].astype(BF16)

    @pl.when(slab == 3)
    def _():
        out_s[...] = dot_tt(dq_s[...], wq_ref[...]) + dot_tt(dk_s[...], wk_ref[...]) + dot_tt(dv_s[...], wv_ref[...])
        half = REST // 2
        keep_ref[...] = out_s[pl.ds(pl.multiple_of(head * half, half), half), :]
        send_ref[...] = out_s[pl.ds(pl.multiple_of((1 - head) * half, half), half), :].astype(BF16)


def dil_kernel(place_ref, perm_ref, got_ref, dil_ref, wq_ref, wk_ref, wv_ref, keep_ref, send_ref, out_s):
    head = place_ref[1]

    def both(pieces):
        return jnp.concatenate(pieces, axis=1)

    dk = both([got_ref[h, :DIL, :64].astype(F32) for h in range(HEADS)])
    dv = both([got_ref[h, :DIL, 64:].astype(F32) for h in range(HEADS)])
    dq = jnp.concatenate(
        [both([got_ref[h, DIL:, s * 64 : s * 64 + 64].astype(F32) for h in range(HEADS)]) for s in range(2)], axis=0
    )
    perm = perm_ref[...]
    out = None
    for grad, i, w_ref in ((dq, 0, wq_ref), (dk, 1, wk_ref), (dv, 2, wv_ref)):
        rows = dot(perm, (grad + dil_ref[i]).astype(BF16)).astype(BF16)
        part = dot_tt(rows, w_ref[...])
        out = part if out is None else out + part
    out_s[...] = out
    half = DIL // 2
    keep_ref[...] = out_s[pl.ds(pl.multiple_of(head * half, half), half), :]
    send_ref[...] = out_s[pl.ds(pl.multiple_of((1 - head) * half, half), half), :].astype(BF16)


def last_kernel(perm_ref, keep_d, got_d, keep_r, got_r, out_ref):
    rows = jnp.concatenate(
        [keep_d[...] + got_d[...].astype(F32), keep_r[...] + got_r[...].astype(F32)], axis=0
    ).astype(BF16)
    out_ref[...] = dot(perm_ref[...], rows).astype(BF16)


def params():
    return pltpu.CompilerParams(vmem_limit_bytes=VMEM)


def cost(flops, bytes_accessed, exps):
    return pl.CostEstimate(flops=flops, bytes_accessed=bytes_accessed, transcendentals=exps)


def shape(dims, dtype):
    return jax.ShapeDtypeStruct(dims, dtype)


def slab_spec(rows):
    return pl.BlockSpec((rows, LANES), lambda s: (0, s))


def whole(dims):
    return pl.BlockSpec(dims, lambda s: (0,) * len(dims))


def swap(x, axis, bits):
    return lax.ppermute(x, axis, [(i, i ^ bits) for i in range(lax.axis_size(axis))])


def on_device(queries, keys, values, grad_attn, w_query, w_key, w_value):
    size = lax.axis_size("tm")
    lines = [[a * 8 + j for j in range(8)] for a in range(size // 8)]
    across = [[b * 64 + a * 8 + j for a in range(8)] for b in range(size // 64) for j in range(8)]
    smem = pl.BlockSpec(memory_space=pltpu.SMEM)
    place = jnp.stack([lax.rem(lax.axis_index("tm"), 8), lax.axis_index("head")]).astype(jnp.int32)
    dil, order = frame_order()
    perm = jnp.asarray(one_hot(order, ROWS), BF16)
    perm_dil = jnp.asarray(one_hot(np.argsort(dil), DIL), BF16)
    f = np.arange(256)
    seat = np.where(f % 4 == 0, f // 4, 64 + f - f // 4 - 1)
    perm_last = jnp.asarray(one_hot(seat, 256), BF16)

    block = shape((ROWS, 512), BF16)
    qp, kp, vp, gp, sent = pl.pallas_call(
        pack_kernel,
        grid=(4,),
        in_specs=[whole((ROWS, ROWS))] + [slab_spec(ROWS)] * 4,
        out_specs=[slab_spec(ROWS)] * 4 + [pl.BlockSpec((2, DIL + STAT_ROWS, 256), lambda s: (s, 0, 0))],
        out_shape=[block] * 4 + [shape((HEADS, DIL + STAT_ROWS, 256), BF16)],
        compiler_params=params(),
        name="pack",
    )(perm, queries, keys, values, grad_attn)

    x = lax.all_to_all(sent, "tm", 0, 0, axis_index_groups=lines, tiled=True)
    dq1, dk1, dv1 = pl.pallas_call(
        local_kernel,
        grid=(4,),
        in_specs=[slab_spec(ROWS)] * 4,
        out_specs=[slab_spec(REST), slab_spec(ROWS), slab_spec(ROWS)],
        out_shape=[shape((REST, 512), BF16), shape((ROWS, 512), F32), shape((ROWS, 512), F32)],
        compiler_params=params(),
        cost_estimate=cost(12_000_000_000, 5_000_000, 1_600_000),
        name="local",
    )(qp, kp, vp, gp)

    p16 = swap(x[:, :32, :LANES].reshape(256, LANES), "tm", 8)
    mine64 = x[:, :8, :LANES].reshape(64, LANES)
    c64 = lax.all_to_all(jnp.broadcast_to(mine64, (8, 64, LANES)), "tm", 0, 0, axis_index_groups=across, tiled=True)
    own, dq_own, part16, part64, stat = pl.pallas_call(
        head_kernel,
        out_shape=[
            shape((HEADS, DIL, LANES), F32),
            shape((HEADS, DIL, LANES), F32),
            shape((256, LANES), BF16),
            shape((8, 64, LANES), BF16),
            shape((2, HEADS, DIL), F32),
        ],
        compiler_params=params(),
        name="heads",
    )(x, p16, c64)

    st = stat[None]
    for bit in (1, 2, 4):
        st = jnp.concatenate([st, swap(st, "tm", bit)], axis=0)
    got16 = swap(part16, "tm", 8)
    got64 = lax.all_to_all(part64, "tm", 0, 0, axis_index_groups=across, tiled=True)
    back = pl.pallas_call(
        gather_kernel,
        out_shape=shape((HEADS, DIL + 64, LANES), BF16),
        compiler_params=params(),
        name="gather",
    )(own, dq_own, got16, got64)
    got = lax.all_to_all(back, "tm", 0, 0, axis_index_groups=lines, tiled=True)

    half = REST // 2
    dil_own, keep_r, send_r = pl.pallas_call(
        rest_kernel,
        grid=(4,),
        in_specs=[smem]
        + [slab_spec(ROWS)] * 4
        + [slab_spec(REST), slab_spec(ROWS), slab_spec(ROWS), whole((8, 2, HEADS, DIL))]
        + [whole((1024, 512))] * 3,
        out_specs=[pl.BlockSpec((3, DIL, LANES), lambda s: (0, 0, s)), whole((half, 1024)), whole((half, 1024))],
        out_shape=[shape((3, DIL, 512), F32), shape((half, 1024), F32), shape((half, 1024), BF16)],
        scratch_shapes=[pltpu.VMEM((REST, 512), BF16)] * 3 + [pltpu.VMEM((REST, 1024), F32)],
        compiler_params=params(),
        cost_estimate=cost(5_000_000_000, 9_000_000, 600_000),
        name="rest",
    )(place, qp, kp, vp, gp, dq1, dk1, dv1, st, w_query, w_key, w_value)
    got_r = swap(send_r, "head", 1)

    vmem = pl.BlockSpec(memory_space=pltpu.VMEM)
    keep_d, send_d = pl.pallas_call(
        dil_kernel,
        in_specs=[smem] + [vmem] * 6,
        out_shape=[shape((DIL // 2, 1024), F32), shape((DIL // 2, 1024), BF16)],
        scratch_shapes=[pltpu.VMEM((DIL, 1024), F32)],
        compiler_params=params(),
        name="dil",
    )(place, perm_dil, got, dil_own, w_query, w_key, w_value)
    got_d = swap(send_d, "head", 1)
    return pl.pallas_call(
        last_kernel,
        out_shape=shape((256, 1024), BF16),
        compiler_params=params(),
        name="last",
    )(perm_last, keep_d, got_d, keep_r, got_r)


def solution(mesh):
    return jax.shard_map(
        on_device,
        mesh=mesh,
        in_specs=(
            P("tm", "head"),
            P("tm", "head"),
            P("tm", "head"),
            P("tm", "head"),
            P(None, "head"),
            P(None, "head"),
            P(None, "head"),
        ),
        out_specs=P(("tm", "head"), None),
        check_vma=False,
    )
```

```python
import functools

import jax
import jax.numpy as jnp
import numpy as np
from jax import lax
from jax.experimental import pallas as pl
from jax.experimental.pallas import tpu as pltpu
from jax.sharding import PartitionSpec as P

BF16 = jnp.bfloat16
F32 = jnp.float32
ROWS = 512
DIL = 128
REST = ROWS - DIL
LANES = 128
HEADS = 8
STAT_ROWS = 16
MIB = 1024 * 1024
LARGE = 62 * MIB
TALL = 20 * 1024
LOW = -1e30


def frame_order():
    r = np.arange(DIL)
    dil = np.concatenate([r[r % 16 == 0], r[(r % 4 == 0) & (r % 16 != 0)], r[r % 4 != 0]])
    f = np.arange(ROWS)
    return dil, np.concatenate([dil * 4, f[f % 4 != 0]])


def one_hot(index, width):
    out = np.zeros((len(index), width), np.float32)
    out[np.arange(len(index)), index] = 1
    return out


def order_hot():
    p = lax.broadcasted_iota(jnp.int32, (ROWS, LANES), 0)

    def skip(i):
        return i + lax.shift_right_logical(i * 171, 9) + 1

    frame = jnp.where(
        p < 8,
        64 * p,
        jnp.where(p < 32, 16 * skip(p - 8), jnp.where(p < DIL, 4 * skip(p - 32), skip(p - DIL))),
    )
    lane = lax.broadcasted_iota(jnp.int32, (ROWS, LANES), 1)
    return jnp.concatenate(
        [jnp.where(frame == lane + i * LANES, 1.0, 0.0).astype(BF16) for i in range(ROWS // LANES)], axis=1
    )


def dot_tt(a, b):
    return lax.dot_general(a, b, (((1,), (1,)), ((), ())), preferred_element_type=F32)


def dot(a, b):
    return jnp.dot(a, b, preferred_element_type=F32)


def half_mask(side):
    lane = lax.broadcasted_iota(jnp.int32, (1, LANES), 1)
    return jnp.where((lane >= 64) == (side == 1), 1.0, 0.0)


def pair(x):
    return jnp.concatenate([x * half_mask(0).astype(BF16), x * half_mask(1).astype(BF16)], axis=0)


def choose(first, second):
    lane = lax.broadcasted_iota(jnp.int32, first.shape, 1)
    return jnp.where(lane < 64, first, second)


def stats(scores, grad_prob):
    top = jnp.max(scores, axis=0, keepdims=True)
    e = jnp.exp(scores - top)
    total = jnp.sum(e, axis=0, keepdims=True)
    delta = jnp.sum(e * grad_prob, axis=0, keepdims=True) / total
    return e, total, top + jnp.log(total), delta


def thirds(x):
    a = x.astype(BF16).astype(F32)
    b = (x - a).astype(BF16).astype(F32)
    return [a, b, x - a - b]


def pack_kernel(perm_hbm, q_hbm, k_hbm, v_hbm, g_hbm, x_hbm, perm_ref, in_ref, x_ref, sems, out_sems, perm_sem):
    def fetch(s, i):
        cols = pl.ds(s * LANES, LANES)
        source = (q_hbm, k_hbm, v_hbm, g_hbm)[i]
        return pltpu.make_async_copy(source.at[:, cols], in_ref.at[s, i], sems.at[s, i])

    def put(s):
        return pltpu.make_async_copy(x_ref.at[pl.ds(2 * s, 2)], x_hbm.at[pl.ds(2 * s, 2)], out_sems.at[s])

    perm_copy = pltpu.make_async_copy(perm_hbm, perm_ref, perm_sem)
    perm_copy.start()
    for s in range(4):
        for i in range(4):
            fetch(s, i).start()
    perm_copy.wait()
    for s in range(4):
        for i in range(4):
            fetch(s, i).wait()
        k, v = in_ref[s, 1], in_ref[s, 2]
        block = jnp.concatenate([in_ref[s, 0] * BF16(0.125), k, v, in_ref[s, 3]], axis=1)
        block = dot(perm_ref[...], block).astype(BF16)
        qd, kd, vd, gd = (block[:, i * LANES : (i + 1) * LANES] for i in range(4))
        scores = dot_tt(k, pair(qd))
        grad_prob = dot_tt(v, pair(gd))
        _, _, lse, delta = stats(scores, grad_prob)
        for h in range(2):
            part = slice(h * DIL, (h + 1) * DIL)
            rows = thirds(lse[:, part]) + thirds(delta[:, part])
            rows = jnp.concatenate(rows + [jnp.zeros((STAT_ROWS - 6, LANES), F32)], axis=0)
            cols = slice(h * 64, h * 64 + 64)
            x_ref[2 * s + h, :DIL, :] = jnp.concatenate([kd[:, cols], vd[:, cols], qd[:, cols], gd[:, cols]], axis=1)
            x_ref[2 * s + h, DIL:, :] = jnp.concatenate([rows, jnp.zeros_like(rows)], axis=1).astype(BF16)
        put(s).start()
    for s in range(4):
        put(s).wait()


def local_kernel(perm_ref, q_ref, k_ref, v_ref, g_ref, in_ref, dq_ref, sum_ref, token_ref):
    token_ref[...] = jnp.zeros_like(token_ref)
    block = jnp.concatenate([q_ref[...] * BF16(0.125), g_ref[...]], axis=1)
    block = dot(perm_ref[...], block).astype(BF16)
    in_ref[0] = block[:DIL, :LANES]
    in_ref[1] = block[:DIL, LANES:]
    q, g = block[DIL:, :LANES], block[DIL:, LANES:]
    k, v = k_ref[...], v_ref[...]
    q2, g2 = pair(q), pair(g)
    scores = dot_tt(k, q2)
    grad_prob = dot_tt(v, g2)
    e, total, _, delta = stats(scores, grad_prob)
    p = e * (1.0 / total)
    ds = (p * (grad_prob - delta)).astype(BF16)
    dq = dot((k * BF16(0.125)).T, ds)
    dq_ref[...] = jnp.concatenate([dq[:64, :REST], dq[64:, REST:]], axis=0).T.astype(BF16)
    sum_ref[0] = dot(ds, q2).astype(BF16)
    sum_ref[1] = dot(p.astype(BF16), g2).astype(BF16)


def pick16_kernel(x_ref, _, b16_ref):
    b16_ref[...] = x_ref[:, :32, :LANES].reshape(256, LANES)


def pick64_kernel(b16_ref, b64_ref):
    rows = b16_ref[...].reshape(HEADS, 32, LANES)[:, :16].astype(F32)[:, :8].reshape(64, LANES).astype(BF16)
    for a in range(HEADS):
        b64_ref[a] = rows


def head_kernel(x_ref, p16_ref, c64_ref, own_ref, dq_ref, part16_ref, part64_ref, stat_ref):
    def products(kv, qg):
        both = dot_tt(kv, pair(qg))
        return both[:, : qg.shape[0]], both[:, qg.shape[0] :]

    def grads(kv, qg, scores, grad_prob, lse, delta):
        p = jnp.exp(scores - lse)
        ds = (p * (grad_prob - delta)).astype(BF16)
        dkv = dot(jnp.concatenate([ds, p.astype(BF16)], axis=1), pair(qg))
        dq = dot((kv * BF16(0.125)).T, ds).T
        return dkv, dq

    def spread(row, width, fill):
        lines = []
        for s in range(HEADS):
            piece = row[:, s * width : (s + 1) * width]
            if width < DIL:
                piece = jnp.concatenate([piece, jnp.full((1, DIL - width), fill, F32)], axis=1)
            lines.append(piece)
        return jnp.concatenate(lines, axis=0)

    def collect(table, width):
        return jnp.concatenate([table[s : s + 1, :width] for s in range(HEADS)], axis=1)

    segments = []
    for s in range(2):
        block = x_ref[4 * s : 4 * s + 4, :DIL, :].reshape(4 * DIL, 2 * LANES)
        segments.append((block[:, :LANES], block[:, LANES:]))
    block16 = x_ref[:, :32, :].reshape(256, 2 * LANES)
    kv16 = jnp.concatenate([block16[:, :LANES], p16_ref[...]], axis=0)
    qg16 = block16[:, LANES:]
    qg64 = x_ref[:, :16, LANES:].astype(F32)[:, :8, :].reshape(64, LANES).astype(BF16)
    kv64 = c64_ref[...].reshape(512, LANES)

    lse1, delta1 = [], []
    for s in range(HEADS):
        rows = x_ref[s, DIL:, :LANES].astype(F32)
        lse1.append(rows[0:1] + rows[1:2] + rows[2:3])
        delta1.append(rows[3:4] + rows[4:5] + rows[5:6])
    lses = [jnp.concatenate(lse1, axis=0)]
    deltas = [jnp.concatenate(delta1, axis=0)]

    made = [products(kv, qg) for kv, qg in segments]
    got = [stats(*pair) for pair in made]
    lses.append(spread(jnp.concatenate([got[0][2], got[1][2]], axis=1), DIL, LOW))
    deltas.append(spread(jnp.concatenate([got[0][3], got[1][3]], axis=1), DIL, 0.0))
    made16 = products(kv16, qg16)
    got = stats(*made16)
    lses.append(spread(got[2], 32, LOW))
    deltas.append(spread(got[3], 32, 0.0))
    made64 = products(kv64, qg64)
    got = stats(*made64)
    lses.append(spread(got[2], 8, LOW))
    deltas.append(spread(got[3], 8, 0.0))

    top = functools.reduce(jnp.maximum, lses)
    parts = [jnp.exp(x - top) for x in lses]
    total = sum(parts)
    lse = top + jnp.log(total)
    delta = sum(w * d for w, d in zip(parts, deltas)) / total
    stat_ref[0] = lse
    stat_ref[1] = delta

    for s in range(2):
        row = [jnp.concatenate([t[4 * s + i : 4 * s + i + 1] for i in range(4)], axis=1) for t in (lse, delta)]
        dkv, dq = grads(*segments[s], *made[s], *row)
        own_ref[4 * s : 4 * s + 4] = dkv.reshape(4, DIL, LANES)
        dq_ref[4 * s : 4 * s + 4] = dq.reshape(4, DIL, LANES)
    dkv, dq = grads(kv16, qg16, *made16, collect(lse, 32), collect(delta, 32))
    own_ref[:, :32, :] = own_ref[:, :32, :] + dkv[:256].reshape(HEADS, 32, LANES)
    part16_ref[...] = dkv[256:].astype(BF16)
    dq_ref[:, :32, :] = dq_ref[:, :32, :] + dq.reshape(HEADS, 32, LANES)
    dkv, dq = grads(kv64, qg64, *made64, collect(lse, 8), collect(delta, 8))
    part64_ref[...] = dkv.reshape(HEADS, 64, LANES).astype(BF16)
    dq_ref[:, :8, :] = dq_ref[:, :8, :] + dq.reshape(HEADS, 8, LANES)


def gather_kernel(own_ref, dq_ref, got16_ref, got64_ref, out_ref):
    got16 = got16_ref[...].astype(F32).reshape(HEADS, 32, LANES)
    got64 = got64_ref[...].astype(F32)
    got64 = sum(got64[i] for i in range(HEADS)).reshape(HEADS, 8, LANES)
    first = got16[:, :8] + got64
    dkv = own_ref[...]
    dkv = jnp.concatenate([dkv[:, :8] + first, dkv[:, 8:32] + got16[:, 8:], dkv[:, 32:]], axis=1)
    out_ref[:, :DIL, :] = dkv.astype(BF16)
    for s in range(HEADS):
        dq = dq_ref[s]
        out_ref[s, DIL:, :] = jnp.concatenate([dq[:64, :64], dq[64:, :64]], axis=1).astype(BF16)


def rest_kernel(
    st_hbm, in_hbm, k_hbm, v_hbm, sum_hbm, dq_hbm, wq_hbm, wk_hbm, wv_hbm,
    dil_ref, keep_ref, send_ref, w_hbm,
    st_ref, in_ref, k_ref, v_ref, sum_ref, dq_s, w_s, dk_s, dv_s, sems, out_sems,
):
    pairs = [(st_hbm, st_ref), (in_hbm, in_ref), (k_hbm, k_ref), (v_hbm, v_ref), (sum_hbm, sum_ref)]
    pairs += [(dq_hbm, dq_s)]
    pairs += [(w, w_s.at[i]) for i, w in enumerate((wq_hbm, wk_hbm, wv_hbm))]
    fetches = [pltpu.make_async_copy(a, b, sems.at[i]) for i, (a, b) in enumerate(pairs)]
    for fetch in fetches:
        fetch.start()
    line = lax.rem(lax.axis_index("tm"), 8)
    head = lax.axis_index("head")
    perm = order_hot()
    for fetch in fetches[:4]:
        fetch.wait()
    for slab in range(4):
        cols = slice(slab * LANES, (slab + 1) * LANES)
        k, v = k_ref[:, cols], v_ref[:, cols]
        q2, g2 = pair(in_ref[0, :, cols]), pair(in_ref[1, :, cols])
        scores = dot_tt(k, q2)
        grad_prob = dot_tt(v, g2)
        lse, delta = [], []
        for h in range(2):
            at = jnp.bitwise_xor(2 * slab + h, line)
            lse.append(st_ref[at, 0, pl.ds(line, 1), :])
            delta.append(st_ref[at, 1, pl.ds(line, 1), :])
        p = jnp.exp(scores - jnp.concatenate(lse, axis=1))
        ds = (p * (grad_prob - jnp.concatenate(delta, axis=1))).astype(BF16)
        dq = dot((k * BF16(0.125)).T, ds)
        dil_ref[0, :, cols] = jnp.concatenate([dq[:64, :DIL], dq[64:, DIL:]], axis=0).T.astype(BF16)
        dk, dv = dot(ds, q2), dot(p.astype(BF16), g2)
        if slab == 0:
            fetches[4].wait()
        dkv = [dk + sum_ref[0, :, cols].astype(F32), dv + sum_ref[1, :, cols].astype(F32)]
        moved = dot(perm, jnp.concatenate(dkv, axis=1).astype(BF16)).astype(BF16)
        dil_ref[1, :, cols] = moved[:DIL, :LANES]
        dil_ref[2, :, cols] = moved[:DIL, LANES:]
        dk_s[:, cols] = moved[DIL:, :LANES]
        dv_s[:, cols] = moved[DIL:, LANES:]
    for fetch in fetches[5:]:
        fetch.wait()
    puts = [pltpu.make_async_copy(w_s.at[i], w_hbm.at[i, pl.ds(0, 1024)], out_sems.at[i]) for i in range(3)]
    for put in puts:
        put.start()
    half = REST // 2
    keep = pl.ds(pl.multiple_of(head * half, half), half)
    send = pl.ds(pl.multiple_of((1 - head) * half, half), half)
    for i, grad in enumerate((dq_s, dk_s, dv_s)):
        keep_ref[i] = grad[keep, :]
    out = dot_tt(dq_s[send, :], w_s[0]) + dot_tt(dk_s[send, :], w_s[1]) + dot_tt(dv_s[send, :], w_s[2])
    send_ref[...] = out.astype(BF16)
    for put in puts:
        put.wait()


def dil_kernel(perm_ref, got_ref, dil_ref, kept_ref, w_hbm, keep_ref, send_ref, keep_r, out_s, w_s, sems):
    head = lax.axis_index("head")
    fetches = [pltpu.make_async_copy(w_hbm.at[i, pl.ds(0, 1024)], w_s.at[i], sems.at[i]) for i in range(3)]
    for fetch in fetches:
        fetch.start()

    def both(pieces):
        return jnp.concatenate(pieces, axis=1)

    dk = both([got_ref[h, :DIL, :64].astype(F32) for h in range(HEADS)])
    dv = both([got_ref[h, :DIL, 64:].astype(F32) for h in range(HEADS)])
    dq = jnp.concatenate(
        [both([got_ref[h, DIL:, s * 64 : s * 64 + 64].astype(F32) for h in range(HEADS)]) for s in range(2)], axis=0
    )
    perm = perm_ref[...]
    grads = [dot(perm, (grad + dil_ref[i].astype(F32)).astype(BF16)).astype(BF16) for i, grad in enumerate((dq, dk, dv))]
    out = None
    for i, rows in enumerate(grads):
        fetches[i].wait()
        part = dot_tt(jnp.concatenate([rows, kept_ref[i]], axis=0), w_s[i])
        out = part if out is None else out + part
    out_s[...] = out[:DIL]
    keep_r[...] = out[DIL:].astype(BF16)
    half = DIL // 2
    keep_ref[...] = out_s[pl.ds(pl.multiple_of(head * half, half), half), :]
    send_ref[...] = out_s[pl.ds(pl.multiple_of((1 - head) * half, half), half), :].astype(BF16)


def last_kernel(perm_ref, keep_d, got_d, keep_r, got_r, out_ref):
    rows = jnp.concatenate(
        [keep_d[...] + got_d[...].astype(F32), keep_r[...].astype(F32) + got_r[...].astype(F32)], axis=0
    ).astype(BF16)
    out_ref[...] = dot(perm_ref[...], rows).astype(BF16)


def params(limit=LARGE):
    return pltpu.CompilerParams(vmem_limit_bytes=limit)


def cost(flops, bytes_accessed, exps):
    return pl.CostEstimate(flops=flops, bytes_accessed=bytes_accessed, transcendentals=exps)


def shape(dims, dtype):
    return jax.ShapeDtypeStruct(dims, dtype)


def slab_spec(rows):
    return pl.BlockSpec((rows, LANES), lambda s: (0, s))


def whole(dims):
    return pl.BlockSpec(dims, lambda s: (0,) * len(dims))


def swap(x, axis, bits):
    return lax.ppermute(x, axis, [(i, i ^ bits) for i in range(lax.axis_size(axis))])


def on_device(queries, keys, values, grad_attn, w_query, w_key, w_value):
    size = lax.axis_size("tm")
    lines = [[a * 8 + j for j in range(8)] for a in range(size // 8)]
    across = [[b * 64 + a * 8 + j for a in range(8)] for b in range(size // 64) for j in range(8)]
    hbm = pl.BlockSpec(memory_space=pltpu.HBM)
    dil, order = frame_order()
    perm = jnp.asarray(one_hot(order, ROWS), BF16)
    perm_first = jnp.asarray(one_hot(order[:DIL], ROWS), BF16)
    perm_dil = jnp.asarray(one_hot(np.argsort(dil), DIL), BF16)
    f = np.arange(256)
    seat = np.where(f % 4 == 0, f // 4, 64 + f - f // 4 - 1)
    perm_last = jnp.asarray(one_hot(seat, 256), BF16)

    sent = pl.pallas_call(
        pack_kernel,
        in_specs=[hbm] * 5,
        out_specs=hbm,
        out_shape=shape((HEADS, DIL + STAT_ROWS, 256), BF16),
        scratch_shapes=[
            pltpu.VMEM((DIL, ROWS), BF16),
            pltpu.VMEM((4, 4, ROWS, LANES), BF16),
            pltpu.VMEM((HEADS, DIL + STAT_ROWS, 256), BF16),
            pltpu.SemaphoreType.DMA((4, 4)),
            pltpu.SemaphoreType.DMA((4,)),
            pltpu.SemaphoreType.DMA,
        ],
        compiler_params=params(),
        name="pack",
    )(perm_first, queries, keys, values, grad_attn)

    x = lax.all_to_all(sent, "tm", 0, 0, axis_index_groups=lines, tiled=True)

    def stack_spec(planes, rows):
        return pl.BlockSpec((planes, rows, LANES), lambda s: (0, 0, s))

    ins, dq1, sums, token = pl.pallas_call(
        local_kernel,
        grid=(4,),
        in_specs=[whole((ROWS, ROWS))] + [slab_spec(ROWS)] * 4,
        out_specs=[stack_spec(2, DIL), slab_spec(REST), stack_spec(2, ROWS), whole((8, LANES))],
        out_shape=[
            shape((2, DIL, 512), BF16),
            shape((REST, 512), BF16),
            shape((2, ROWS, 512), BF16),
            shape((8, LANES), F32),
        ],
        compiler_params=params(),
        cost_estimate=cost(12_000_000_000, 5_000_000, 1_600_000),
        name="local",
    )(perm, queries, keys, values, grad_attn)

    mine16 = pl.pallas_call(
        pick16_kernel, out_shape=shape((256, LANES), BF16), compiler_params=params(8 * MIB), name="pick16"
    )(x, token)
    p16 = swap(mine16, "tm", 8)
    mine64 = pl.pallas_call(
        pick64_kernel, out_shape=shape((8, 64, LANES), BF16), compiler_params=params(8 * MIB), name="pick64"
    )(mine16)
    c64 = lax.all_to_all(mine64, "tm", 0, 0, axis_index_groups=across, tiled=True)
    own, dq_own, part16, part64, stat = pl.pallas_call(
        head_kernel,
        out_shape=[
            shape((HEADS, DIL, LANES), F32),
            shape((HEADS, DIL, LANES), F32),
            shape((256, LANES), BF16),
            shape((8, 64, LANES), BF16),
            shape((2, HEADS, DIL), F32),
        ],
        compiler_params=params(24 * MIB),
        name="heads",
    )(x, p16, c64)

    st = stat[None]
    for bit in (1, 2, 4):
        st = jnp.concatenate([st, swap(st, "tm", bit)], axis=0)
    got16 = swap(part16, "tm", 8)
    got64 = lax.all_to_all(part64, "tm", 0, 0, axis_index_groups=across, tiled=True)
    back = pl.pallas_call(
        gather_kernel,
        out_shape=shape((HEADS, DIL + 64, LANES), BF16),
        compiler_params=params(8 * MIB),
        name="gather",
    )(own, dq_own, got16, got64)
    got = lax.all_to_all(back, "tm", 0, 0, axis_index_groups=lines, tiled=True)

    vmem = pl.BlockSpec(memory_space=pltpu.VMEM)
    half = REST // 2
    dil_own, kept, send_r, weights = pl.pallas_call(
        rest_kernel,
        in_specs=[hbm] * 9,
        out_specs=[pl.BlockSpec(memory_space=pltpu.VMEM)] * 3 + [hbm],
        out_shape=[
            shape((3, DIL, 512), BF16),
            shape((3, half, 512), BF16),
            shape((half, 1024), BF16),
            shape((3, TALL, 512), BF16),
        ],
        scratch_shapes=[
            pltpu.VMEM((8, 2, HEADS, DIL), F32),
            pltpu.VMEM((2, DIL, 512), BF16),
            pltpu.VMEM((ROWS, 512), BF16),
            pltpu.VMEM((ROWS, 512), BF16),
            pltpu.VMEM((2, ROWS, 512), BF16),
            pltpu.VMEM((REST, 512), BF16),
            pltpu.VMEM((3, 1024, 512), BF16),
            pltpu.VMEM((REST, 512), BF16),
            pltpu.VMEM((REST, 512), BF16),
            pltpu.SemaphoreType.DMA((9,)),
            pltpu.SemaphoreType.DMA((3,)),
        ],
        compiler_params=params(),
        cost_estimate=cost(5_000_000_000, 9_000_000, 600_000),
        name="rest",
    )(st, ins, keys, values, sums, dq1, w_query, w_key, w_value)
    got_r = swap(send_r, "head", 1)

    keep_d, send_d, keep_r = pl.pallas_call(
        dil_kernel,
        in_specs=[vmem] * 4 + [hbm],
        out_shape=[shape((DIL // 2, 1024), F32), shape((DIL // 2, 1024), BF16), shape((half, 1024), BF16)],
        scratch_shapes=[
            pltpu.VMEM((DIL, 1024), F32),
            pltpu.VMEM((3, 1024, 512), BF16),
            pltpu.SemaphoreType.DMA((3,)),
        ],
        compiler_params=params(12 * MIB),
        name="dil",
    )(perm_dil, got, dil_own, kept, weights)
    got_d = swap(send_d, "head", 1)
    return pl.pallas_call(
        last_kernel,
        out_shape=shape((256, 1024), BF16),
        compiler_params=params(8 * MIB),
        name="last",
    )(perm_last, keep_d, got_d, keep_r, got_r)


def solution(mesh):
    return jax.shard_map(
        on_device,
        mesh=mesh,
        in_specs=(
            P("tm", "head"),
            P("tm", "head"),
            P("tm", "head"),
            P("tm", "head"),
            P(None, "head"),
            P(None, "head"),
            P(None, "head"),
        ),
        out_specs=P(("tm", "head"), None),
        check_vma=False,
    )
```

```python
import functools

import jax
import jax.numpy as jnp
import numpy as np
from jax import lax
from jax.experimental import pallas as pl
from jax.experimental.pallas import tpu as pltpu
from jax.sharding import PartitionSpec as P

BF16 = jnp.bfloat16
F32 = jnp.float32
ROWS = 512
DIL = 128
REST = ROWS - DIL
LANES = 128
HEADS = 8
STAT_ROWS = 16
OWN = 1024
PASSED = DIL + REST // 2
MIB = 1024 * 1024
LARGE = 62 * MIB
TALL = 15 * 1024
LOW = -1e30


def frame_order():
    r = np.arange(DIL)
    dil = np.concatenate([r[r % 16 == 0], r[(r % 4 == 0) & (r % 16 != 0)], r[r % 4 != 0]])
    f = np.arange(ROWS)
    return dil, np.concatenate([dil * 4, f[f % 4 != 0]])


def one_hot(index, width):
    out = np.zeros((len(index), width), np.float32)
    out[np.arange(len(index)), index] = 1
    return out


def dot_tt(a, b):
    return lax.dot_general(a, b, (((1,), (1,)), ((), ())), preferred_element_type=F32)


def dot(a, b):
    return jnp.dot(a, b, preferred_element_type=F32)


def half_mask(side):
    lane = lax.broadcasted_iota(jnp.int32, (1, LANES), 1)
    return jnp.where((lane >= 64) == (side == 1), 1.0, 0.0)


def pair(x):
    return jnp.concatenate([x * half_mask(0).astype(BF16), x * half_mask(1).astype(BF16)], axis=0)


def choose(first, second):
    lane = lax.broadcasted_iota(jnp.int32, first.shape, 1)
    return jnp.where(lane < 64, first, second)


def stats(scores, grad_prob):
    top = jnp.max(scores, axis=0, keepdims=True)
    e = jnp.exp(scores - top)
    total = jnp.sum(e, axis=0, keepdims=True)
    delta = jnp.sum(e * grad_prob, axis=0, keepdims=True) / total
    return e, total, top + jnp.log(total), delta


def thirds(x):
    a = x.astype(BF16).astype(F32)
    b = (x - a).astype(BF16).astype(F32)
    return [a, b, x - a - b]


def pack_kernel(perm_hbm, q_hbm, k_hbm, v_hbm, g_hbm, x_hbm, perm_ref, in_ref, x_ref, sems, out_sems, perm_sem):
    def fetch(s, i):
        cols = pl.ds(s * LANES, LANES)
        source = (q_hbm, k_hbm, v_hbm, g_hbm)[i]
        return pltpu.make_async_copy(source.at[:, cols], in_ref.at[s, i], sems.at[s, i])

    def put(s):
        return pltpu.make_async_copy(x_ref.at[pl.ds(2 * s, 2)], x_hbm.at[pl.ds(2 * s, 2)], out_sems.at[s])

    perm_copy = pltpu.make_async_copy(perm_hbm, perm_ref, perm_sem)
    perm_copy.start()
    for s in range(4):
        for i in range(4):
            fetch(s, i).start()
    perm_copy.wait()
    for s in range(4):
        for i in range(4):
            fetch(s, i).wait()
    for s in range(4):
        k, v = in_ref[s, 1], in_ref[s, 2]
        block = jnp.concatenate([in_ref[s, 0] * BF16(0.125), k, v, in_ref[s, 3]], axis=1)
        block = dot(perm_ref[...], block).astype(BF16)
        qd, kd, vd, gd = (block[:, i * LANES : (i + 1) * LANES] for i in range(4))
        scores = dot_tt(k, pair(qd))
        grad_prob = dot_tt(v, pair(gd))
        _, _, lse, delta = stats(scores, grad_prob)
        for h in range(2):
            part = slice(h * DIL, (h + 1) * DIL)
            rows = thirds(lse[:, part]) + thirds(delta[:, part])
            rows = jnp.concatenate(rows + [jnp.zeros((STAT_ROWS - 6, LANES), F32)], axis=0)
            cols = slice(h * 64, h * 64 + 64)
            x_ref[2 * s + h, :DIL, :] = jnp.concatenate([kd[:, cols], vd[:, cols], qd[:, cols], gd[:, cols]], axis=1)
            x_ref[2 * s + h, DIL:, :] = jnp.concatenate([rows, jnp.zeros_like(rows)], axis=1).astype(BF16)
    for s in range(4):
        put(s).start()
    for s in range(4):
        put(s).wait()


def local_kernel(
    perm_ref, q_ref, k_ref, v_ref, g_ref, wq_hbm, wk_hbm, wv_hbm,
    in_ref, kv_ref, dq_ref, sum_ref, w_hbm, w_s, sems,
):
    step = pl.program_id(0)
    loads = [pltpu.make_async_copy(w, w_s.at[i], sems.at[i]) for i, w in enumerate((wq_hbm, wk_hbm, wv_hbm))]
    store = pltpu.make_async_copy(w_s, w_hbm.at[:, pl.ds(0, OWN)], sems.at[3])

    @pl.when(step == 0)
    def _():
        for load in loads:
            load.start()

    @pl.when(step == 2)
    def _():
        for load in loads:
            load.wait()
        store.start()

    block = jnp.concatenate([q_ref[...] * BF16(0.125), g_ref[...], k_ref[...], v_ref[...]], axis=1)
    block = dot(perm_ref[...], block).astype(BF16)
    in_ref[0] = block[:DIL, :LANES]
    in_ref[1] = block[:DIL, LANES : 2 * LANES]
    q, g = block[DIL:, :LANES], block[DIL:, LANES : 2 * LANES]
    k, v = block[:, 2 * LANES : 3 * LANES], block[:, 3 * LANES :]
    kv_ref[0] = k
    kv_ref[1] = v
    q2, g2 = pair(q), pair(g)
    scores = dot_tt(k, q2)
    grad_prob = dot_tt(v, g2)
    e, total, _, delta = stats(scores, grad_prob)
    p = e * (1.0 / total)
    ds = (p * (grad_prob - delta)).astype(BF16)
    dq = dot((k * BF16(0.125)).T, ds)
    dq_ref[...] = jnp.concatenate([dq[:64, :REST], dq[64:, REST:]], axis=0).T.astype(BF16)
    sum_ref[0] = dot(ds, q2).astype(BF16)
    sum_ref[1] = dot(p.astype(BF16), g2).astype(BF16)

    @pl.when(step == 3)
    def _():
        store.wait()


def pick_kernel(x_ref, _, b16_ref, b64_ref):
    b16_ref[...] = x_ref[:, :32, :LANES].reshape(256, LANES)
    rows = x_ref[:, :16, :LANES].astype(F32)[:, :8, :].reshape(64, LANES).astype(BF16)
    for a in range(HEADS):
        b64_ref[a] = rows


def head_kernel(x_ref, p16_ref, c64_ref, own_ref, dq_ref, part16_ref, part64_ref, stat_ref):
    def products(kv, qg):
        both = dot_tt(kv, pair(qg))
        return both[:, : qg.shape[0]], both[:, qg.shape[0] :]

    def grads(kv, qg, scores, grad_prob, lse, delta):
        p = jnp.exp(scores - lse)
        ds = (p * (grad_prob - delta)).astype(BF16)
        dkv = dot(jnp.concatenate([ds, p.astype(BF16)], axis=1), pair(qg))
        dq = dot((kv * BF16(0.125)).T, ds).T
        return dkv, dq

    def spread(row, width, fill):
        lines = []
        for s in range(HEADS):
            piece = row[:, s * width : (s + 1) * width]
            if width < DIL:
                piece = jnp.concatenate([piece, jnp.full((1, DIL - width), fill, F32)], axis=1)
            lines.append(piece)
        return jnp.concatenate(lines, axis=0)

    def collect(table, width):
        return jnp.concatenate([table[s : s + 1, :width] for s in range(HEADS)], axis=1)

    segments = []
    for s in range(2):
        block = x_ref[4 * s : 4 * s + 4, :DIL, :].reshape(4 * DIL, 2 * LANES)
        segments.append((block[:, :LANES], block[:, LANES:]))
    block16 = x_ref[:, :32, :].reshape(256, 2 * LANES)
    kv16 = jnp.concatenate([block16[:, :LANES], p16_ref[...]], axis=0)
    qg16 = block16[:, LANES:]
    qg64 = x_ref[:, :16, LANES:].astype(F32)[:, :8, :].reshape(64, LANES).astype(BF16)
    kv64 = c64_ref[...].reshape(512, LANES)

    lse1, delta1 = [], []
    for s in range(HEADS):
        rows = x_ref[s, DIL:, :LANES].astype(F32)
        lse1.append(rows[0:1] + rows[1:2] + rows[2:3])
        delta1.append(rows[3:4] + rows[4:5] + rows[5:6])
    lses = [jnp.concatenate(lse1, axis=0)]
    deltas = [jnp.concatenate(delta1, axis=0)]

    made = [products(kv, qg) for kv, qg in segments]
    got = [stats(*pair) for pair in made]
    lses.append(spread(jnp.concatenate([got[0][2], got[1][2]], axis=1), DIL, LOW))
    deltas.append(spread(jnp.concatenate([got[0][3], got[1][3]], axis=1), DIL, 0.0))
    made16 = products(kv16, qg16)
    got = stats(*made16)
    lses.append(spread(got[2], 32, LOW))
    deltas.append(spread(got[3], 32, 0.0))
    made64 = products(kv64, qg64)
    got = stats(*made64)
    lses.append(spread(got[2], 8, LOW))
    deltas.append(spread(got[3], 8, 0.0))

    top = functools.reduce(jnp.maximum, lses)
    parts = [jnp.exp(x - top) for x in lses]
    total = sum(parts)
    lse = top + jnp.log(total)
    delta = sum(w * d for w, d in zip(parts, deltas)) / total
    stat_ref[0] = lse
    stat_ref[1] = delta

    for s in range(2):
        row = [jnp.concatenate([t[4 * s + i : 4 * s + i + 1] for i in range(4)], axis=1) for t in (lse, delta)]
        dkv, dq = grads(*segments[s], *made[s], *row)
        own_ref[4 * s : 4 * s + 4] = dkv.reshape(4, DIL, LANES)
        dq_ref[4 * s : 4 * s + 4] = dq.reshape(4, DIL, LANES)
    dkv, dq = grads(kv16, qg16, *made16, collect(lse, 32), collect(delta, 32))
    own_ref[:, :32, :] = own_ref[:, :32, :] + dkv[:256].reshape(HEADS, 32, LANES)
    part16_ref[...] = dkv[256:].astype(BF16)
    dq_ref[:, :32, :] = dq_ref[:, :32, :] + dq.reshape(HEADS, 32, LANES)
    dkv, dq = grads(kv64, qg64, *made64, collect(lse, 8), collect(delta, 8))
    part64_ref[...] = dkv.reshape(HEADS, 64, LANES).astype(BF16)
    dq_ref[:, :8, :] = dq_ref[:, :8, :] + dq.reshape(HEADS, 8, LANES)


def gather_kernel(own_ref, dq_ref, got16_ref, got64_ref, out_ref):
    got16 = got16_ref[...].astype(F32).reshape(HEADS, 32, LANES)
    got64 = got64_ref[...].astype(F32)
    got64 = sum(got64[i] for i in range(HEADS)).reshape(HEADS, 8, LANES)
    first = got16[:, :8] + got64
    dkv = own_ref[...]
    dkv = jnp.concatenate([dkv[:, :8] + first, dkv[:, 8:32] + got16[:, 8:], dkv[:, 32:]], axis=1)
    out_ref[:, :DIL, :] = dkv.astype(BF16)
    for s in range(HEADS):
        dq = dq_ref[s]
        out_ref[s, DIL:, :] = jnp.concatenate([dq[:64, :64], dq[64:, :64]], axis=1).astype(BF16)


def rest_kernel(
    st_hbm, far_hbm, in_hbm, kv_hbm, sum_hbm, dq_hbm, wq_hbm, wk_hbm, wv_hbm, send_ref, out_hbm,
    st_ref, in_ref, kv_ref, sum_ref, dq_s, w_s, dk_s, dv_s, pass_s, sems, out_sem,
):
    pairs = [(st_hbm, st_ref.at[pl.ds(0, 4)]), (far_hbm, st_ref.at[pl.ds(4, 4)])]
    pairs += [(in_hbm, in_ref), (kv_hbm, kv_ref), (sum_hbm, sum_ref), (dq_hbm, dq_s)]
    pairs += [(w, w_s.at[i]) for i, w in enumerate((wq_hbm, wk_hbm, wv_hbm))]
    fetches = [pltpu.make_async_copy(a, b, sems.at[i]) for i, (a, b) in enumerate(pairs)]
    for fetch in fetches:
        fetch.start()
    line = lax.rem(lax.axis_index("tm"), 8)
    head = lax.axis_index("head")
    for fetch in fetches[:4]:
        fetch.wait()
    for slab in range(4):
        cols = slice(slab * LANES, (slab + 1) * LANES)
        k, v = kv_ref[0, :, cols], kv_ref[1, :, cols]
        q2, g2 = pair(in_ref[0, :, cols]), pair(in_ref[1, :, cols])
        scores = dot_tt(k, q2)
        grad_prob = dot_tt(v, g2)
        lse, delta = [], []
        for h in range(2):
            at = jnp.bitwise_xor(2 * slab + h, line)
            lse.append(st_ref[at, 0, pl.ds(line, 1), :])
            delta.append(st_ref[at, 1, pl.ds(line, 1), :])
        p = jnp.exp(scores - jnp.concatenate(lse, axis=1))
        ds = (p * (grad_prob - jnp.concatenate(delta, axis=1))).astype(BF16)
        dq = dot((k * BF16(0.125)).T, ds)
        pass_s[0, :DIL, cols] = jnp.concatenate([dq[:64, :DIL], dq[64:, DIL:]], axis=0).T.astype(BF16)
        dk, dv = dot(ds, q2), dot(p.astype(BF16), g2)
        if slab == 0:
            fetches[4].wait()
        dk = (dk + sum_ref[0, :, cols].astype(F32)).astype(BF16)
        dv = (dv + sum_ref[1, :, cols].astype(F32)).astype(BF16)
        pass_s[1, :DIL, cols] = dk[:DIL]
        pass_s[2, :DIL, cols] = dv[:DIL]
        dk_s[:, cols] = dk[DIL:]
        dv_s[:, cols] = dv[DIL:]
    half = REST // 2
    keep = pl.ds(pl.multiple_of(head * half, half), half)
    send = pl.ds(pl.multiple_of((1 - head) * half, half), half)
    fetches[5].wait()
    for i, grad in enumerate((dq_s, dk_s, dv_s)):
        pass_s[i, DIL:, :] = grad[keep, :]
    put = pltpu.make_async_copy(pass_s, out_hbm.at[:, pl.ds(0, PASSED)], out_sem)
    put.start()
    for fetch in fetches[6:]:
        fetch.wait()
    out = dot_tt(dq_s[send, :], w_s[0]) + dot_tt(dk_s[send, :], w_s[1]) + dot_tt(dv_s[send, :], w_s[2])
    send_ref[...] = out.astype(BF16)
    put.wait()


def dil_kernel(perm_ref, got_ref, pass_hbm, w_hbm, keep_ref, send_ref, keep_r, out_s, pass_s, w_s, sems):
    head = lax.axis_index("head")
    fetches = [pltpu.make_async_copy(pass_hbm.at[:, pl.ds(0, PASSED)], pass_s, sems.at[3])]
    fetches += [pltpu.make_async_copy(w_hbm.at[i, pl.ds(0, OWN)], w_s.at[i], sems.at[i]) for i in range(3)]
    for fetch in fetches:
        fetch.start()

    def both(pieces):
        return jnp.concatenate(pieces, axis=1)

    dk = both([got_ref[h, :DIL, :64].astype(F32) for h in range(HEADS)])
    dv = both([got_ref[h, :DIL, 64:].astype(F32) for h in range(HEADS)])
    dq = jnp.concatenate(
        [both([got_ref[h, DIL:, s * 64 : s * 64 + 64].astype(F32) for h in range(HEADS)]) for s in range(2)], axis=0
    )
    perm = perm_ref[...]
    fetches[0].wait()
    grads = [dot(perm, (grad + pass_s[i, :DIL, :].astype(F32)).astype(BF16)).astype(BF16) for i, grad in enumerate((dq, dk, dv))]
    out = None
    for i, rows in enumerate(grads):
        fetches[1 + i].wait()
        part = dot_tt(jnp.concatenate([rows, pass_s[i, DIL:, :]], axis=0), w_s[i])
        out = part if out is None else out + part
    out_s[...] = out[:DIL]
    keep_r[...] = out[DIL:].astype(BF16)
    half = DIL // 2
    keep_ref[...] = out_s[pl.ds(pl.multiple_of(head * half, half), half), :]
    send_ref[...] = out_s[pl.ds(pl.multiple_of((1 - head) * half, half), half), :].astype(BF16)


def last_kernel(perm_ref, keep_d, got_d, keep_r, got_r, out_ref):
    rows = jnp.concatenate(
        [keep_d[...] + got_d[...].astype(F32), keep_r[...].astype(F32) + got_r[...].astype(F32)], axis=0
    ).astype(BF16)
    out_ref[...] = dot(perm_ref[...], rows).astype(BF16)


def params(limit=LARGE):
    return pltpu.CompilerParams(vmem_limit_bytes=limit)


def cost(flops, bytes_accessed, exps):
    return pl.CostEstimate(flops=flops, bytes_accessed=bytes_accessed, transcendentals=exps)


def shape(dims, dtype):
    return jax.ShapeDtypeStruct(dims, dtype)


def slab_spec(rows):
    return pl.BlockSpec((rows, LANES), lambda s: (0, s))


def whole(dims):
    return pl.BlockSpec(dims, lambda s: (0,) * len(dims))


def swap(x, axis, bits):
    return lax.ppermute(x, axis, [(i, i ^ bits) for i in range(lax.axis_size(axis))])


def on_device(queries, keys, values, grad_attn, w_query, w_key, w_value):
    size = lax.axis_size("tm")
    lines = [[a * 8 + j for j in range(8)] for a in range(size // 8)]
    across = [[b * 64 + a * 8 + j for a in range(8)] for b in range(size // 64) for j in range(8)]
    hbm = pl.BlockSpec(memory_space=pltpu.HBM)
    vmem = pl.BlockSpec(memory_space=pltpu.VMEM)
    dil, order = frame_order()
    perm = jnp.asarray(one_hot(order, ROWS), BF16)
    perm_first = jnp.asarray(one_hot(order[:DIL], ROWS), BF16)
    perm_dil = jnp.asarray(one_hot(np.argsort(dil), DIL), BF16)
    f = np.arange(256)
    seat = np.where(f % 4 == 0, f // 4, 64 + f - f // 4 - 1)
    perm_last = jnp.asarray(one_hot(seat, 256), BF16)

    sent = pl.pallas_call(
        pack_kernel,
        in_specs=[hbm] * 5,
        out_specs=hbm,
        out_shape=shape((HEADS, DIL + STAT_ROWS, 256), BF16),
        scratch_shapes=[
            pltpu.VMEM((DIL, ROWS), BF16),
            pltpu.VMEM((4, 4, ROWS, LANES), BF16),
            pltpu.VMEM((HEADS, DIL + STAT_ROWS, 256), BF16),
            pltpu.SemaphoreType.DMA((4, 4)),
            pltpu.SemaphoreType.DMA((4,)),
            pltpu.SemaphoreType.DMA,
        ],
        compiler_params=params(),
        name="pack",
    )(perm_first, queries, keys, values, grad_attn)

    x = lax.all_to_all(sent, "tm", 0, 0, axis_index_groups=lines, tiled=True)

    def stack_spec(planes, rows):
        return pl.BlockSpec((planes, rows, LANES), lambda s: (0, 0, s))

    ins, kv, dq1, sums, weights = pl.pallas_call(
        local_kernel,
        grid=(4,),
        in_specs=[whole((ROWS, ROWS))] + [slab_spec(ROWS)] * 4 + [hbm] * 3,
        out_specs=[
            stack_spec(2, DIL),
            stack_spec(2, ROWS),
            slab_spec(REST),
            stack_spec(2, ROWS),
            hbm,
        ],
        scratch_shapes=[pltpu.VMEM((3, OWN, 512), BF16), pltpu.SemaphoreType.DMA((4,))],
        out_shape=[
            shape((2, DIL, 512), BF16),
            shape((2, ROWS, 512), BF16),
            shape((REST, 512), BF16),
            shape((2, ROWS, 512), BF16),
            shape((3, TALL, 512), BF16),
        ],
        compiler_params=params(),
        cost_estimate=cost(12_000_000_000, 5_000_000, 1_600_000),
        name="local",
    )(perm, queries, keys, values, grad_attn, w_query, w_key, w_value)

    mine16, mine64 = pl.pallas_call(
        pick_kernel,
        in_specs=[vmem, hbm],
        out_shape=[shape((256, LANES), BF16), shape((8, 64, LANES), BF16)],
        compiler_params=params(32 * MIB),
        name="pick",
    )(x, weights)
    p16 = swap(mine16, "tm", 8)
    c64 = lax.all_to_all(mine64, "tm", 0, 0, axis_index_groups=across, tiled=True)
    own, dq_own, part16, part64, stat = pl.pallas_call(
        head_kernel,
        out_shape=[
            shape((HEADS, DIL, LANES), F32),
            shape((HEADS, DIL, LANES), F32),
            shape((256, LANES), BF16),
            shape((8, 64, LANES), BF16),
            shape((2, HEADS, DIL), F32),
        ],
        compiler_params=params(24 * MIB),
        name="heads",
    )(x, p16, c64)

    st = stat[None]
    for bit in (1, 2):
        st = jnp.concatenate([st, swap(st, "tm", bit)], axis=0)
    st_far = swap(st, "tm", 4)
    got16 = swap(part16, "tm", 8)
    got64 = lax.all_to_all(part64, "tm", 0, 0, axis_index_groups=across, tiled=True)
    back = pl.pallas_call(
        gather_kernel,
        out_shape=shape((HEADS, DIL + 64, LANES), BF16),
        compiler_params=params(8 * MIB),
        name="gather",
    )(own, dq_own, got16, got64)
    got = lax.all_to_all(back, "tm", 0, 0, axis_index_groups=lines, tiled=True)

    half = REST // 2
    send_r, passed = pl.pallas_call(
        rest_kernel,
        in_specs=[hbm] * 9,
        out_specs=[vmem, hbm],
        out_shape=[shape((half, 1024), BF16), shape((3, TALL, 512), BF16)],
        scratch_shapes=[
            pltpu.VMEM((8, 2, HEADS, DIL), F32),
            pltpu.VMEM((2, DIL, 512), BF16),
            pltpu.VMEM((2, ROWS, 512), BF16),
            pltpu.VMEM((2, ROWS, 512), BF16),
            pltpu.VMEM((REST, 512), BF16),
            pltpu.VMEM((3, OWN, 512), BF16),
            pltpu.VMEM((REST, 512), BF16),
            pltpu.VMEM((REST, 512), BF16),
            pltpu.VMEM((3, PASSED, 512), BF16),
            pltpu.SemaphoreType.DMA((9,)),
            pltpu.SemaphoreType.DMA,
        ],
        compiler_params=params(),
        cost_estimate=cost(5_000_000_000, 9_000_000, 600_000),
        name="rest",
    )(st, st_far, ins, kv, sums, dq1, w_query, w_key, w_value)
    got_r = swap(send_r, "head", 1)

    keep_d, send_d, keep_r = pl.pallas_call(
        dil_kernel,
        in_specs=[vmem] * 2 + [hbm] * 2,
        out_shape=[shape((DIL // 2, 1024), F32), shape((DIL // 2, 1024), BF16), shape((half, 1024), BF16)],
        scratch_shapes=[
            pltpu.VMEM((DIL, 1024), F32),
            pltpu.VMEM((3, PASSED, 512), BF16),
            pltpu.VMEM((3, OWN, 512), BF16),
            pltpu.SemaphoreType.DMA((4,)),
        ],
        compiler_params=params(24 * MIB),
        name="dil",
    )(perm_dil, got, passed, weights)
    got_d = swap(send_d, "head", 1)
    return pl.pallas_call(
        last_kernel,
        out_shape=shape((256, 1024), BF16),
        compiler_params=params(8 * MIB),
        name="last",
    )(perm_last, keep_d, got_d, keep_r, got_r)


def solution(mesh):
    return jax.shard_map(
        on_device,
        mesh=mesh,
        in_specs=(
            P("tm", "head"),
            P("tm", "head"),
            P("tm", "head"),
            P("tm", "head"),
            P(None, "head"),
            P(None, "head"),
            P(None, "head"),
        ),
        out_specs=P(("tm", "head"), None),
        check_vma=False,
    )
```

```python
import functools

import jax
import jax.numpy as jnp
import numpy as np
from jax import lax
from jax.experimental import pallas as pl
from jax.experimental.pallas import tpu as pltpu
from jax.sharding import PartitionSpec as P

BF16 = jnp.bfloat16
F32 = jnp.float32
ROWS = 512
DIL = 128
REST = ROWS - DIL
LANES = 128
HEADS = 8
STAT_ROWS = 16
OWN = 1024
PASSED = DIL + REST // 2
MIB = 1024 * 1024
LARGE = 62 * MIB
TALL = 15 * 1024
LOW = -1e30


def frame_order():
    r = np.arange(DIL)
    dil = np.concatenate([r[r % 16 == 0], r[(r % 4 == 0) & (r % 16 != 0)], r[r % 4 != 0]])
    f = np.arange(ROWS)
    return dil, np.concatenate([dil * 4, f[f % 4 != 0]])


def one_hot(index, width):
    out = np.zeros((len(index), width), np.float32)
    out[np.arange(len(index)), index] = 1
    return out


def dot_tt(a, b):
    return lax.dot_general(a, b, (((1,), (1,)), ((), ())), preferred_element_type=F32)


def dot(a, b):
    return jnp.dot(a, b, preferred_element_type=F32)


def half_mask(side):
    lane = lax.broadcasted_iota(jnp.int32, (1, LANES), 1)
    return jnp.where((lane >= 64) == (side == 1), 1.0, 0.0)


def pair(x):
    return jnp.concatenate([x * half_mask(0).astype(BF16), x * half_mask(1).astype(BF16)], axis=0)


def choose(first, second):
    lane = lax.broadcasted_iota(jnp.int32, first.shape, 1)
    return jnp.where(lane < 64, first, second)


def stats(scores, grad_prob):
    top = jnp.max(scores, axis=0, keepdims=True)
    e = jnp.exp(scores - top)
    total = jnp.sum(e, axis=0, keepdims=True)
    delta = jnp.sum(e * grad_prob, axis=0, keepdims=True) / total
    return e, total, top + jnp.log(total), delta


def thirds(x):
    a = x.astype(BF16).astype(F32)
    b = (x - a).astype(BF16).astype(F32)
    return [a, b, x - a - b]


def pack_kernel(perm_hbm, q_hbm, k_hbm, v_hbm, g_hbm, x_hbm, perm_ref, in_ref, x_ref, sems, out_sems, perm_sem):
    def fetch(s, i):
        cols = pl.ds(s * LANES, LANES)
        source = (q_hbm, k_hbm, v_hbm, g_hbm)[i]
        return pltpu.make_async_copy(source.at[:, cols], in_ref.at[s, i], sems.at[s, i])

    def put(s):
        return pltpu.make_async_copy(x_ref.at[pl.ds(2 * s, 2)], x_hbm.at[pl.ds(2 * s, 2)], out_sems.at[s])

    perm_copy = pltpu.make_async_copy(perm_hbm, perm_ref, perm_sem)
    perm_copy.start()
    for s in range(4):
        for i in range(4):
            fetch(s, i).start()
    perm_copy.wait()
    for s in range(4):
        for i in range(4):
            fetch(s, i).wait()
    for s in range(4):
        k, v = in_ref[s, 1], in_ref[s, 2]
        block = jnp.concatenate([in_ref[s, 0] * BF16(0.125), k, v, in_ref[s, 3]], axis=1)
        block = dot(perm_ref[...], block).astype(BF16)
        qd, kd, vd, gd = (block[:, i * LANES : (i + 1) * LANES] for i in range(4))
        scores = dot_tt(k, pair(qd))
        grad_prob = dot_tt(v, pair(gd))
        _, _, lse, delta = stats(scores, grad_prob)
        for h in range(2):
            part = slice(h * DIL, (h + 1) * DIL)
            rows = thirds(lse[:, part]) + thirds(delta[:, part])
            rows = jnp.concatenate(rows + [jnp.zeros((STAT_ROWS - 6, LANES), F32)], axis=0)
            cols = slice(h * 64, h * 64 + 64)
            x_ref[2 * s + h, :DIL, :] = jnp.concatenate([kd[:, cols], vd[:, cols], qd[:, cols], gd[:, cols]], axis=1)
            x_ref[2 * s + h, DIL:, :] = jnp.concatenate([rows, jnp.zeros_like(rows)], axis=1).astype(BF16)
    for s in range(4):
        put(s).start()
    for s in range(4):
        put(s).wait()


def local_kernel(
    perm_ref, q_ref, k_ref, v_ref, g_ref, wq_hbm, wk_hbm, wv_hbm,
    in_ref, kv_ref, dq_ref, sum_ref, w_hbm, w_s, sems,
):
    step = pl.program_id(0)
    loads = [pltpu.make_async_copy(w, w_s.at[i], sems.at[i]) for i, w in enumerate((wq_hbm, wk_hbm, wv_hbm))]
    store = pltpu.make_async_copy(w_s, w_hbm.at[:, pl.ds(0, OWN)], sems.at[3])

    @pl.when(step == 0)
    def _():
        for load in loads:
            load.start()

    @pl.when(step == 2)
    def _():
        for load in loads:
            load.wait()
        store.start()

    block = jnp.concatenate([q_ref[...] * BF16(0.125), g_ref[...], k_ref[...], v_ref[...]], axis=1)
    block = dot(perm_ref[...], block).astype(BF16)
    in_ref[0] = block[:DIL, :LANES]
    in_ref[1] = block[:DIL, LANES : 2 * LANES]
    q, g = block[DIL:, :LANES], block[DIL:, LANES : 2 * LANES]
    k, v = block[:, 2 * LANES : 3 * LANES], block[:, 3 * LANES :]
    kv_ref[0] = k
    kv_ref[1] = v
    q2, g2 = pair(q), pair(g)
    scores = dot_tt(k, q2)
    grad_prob = dot_tt(v, g2)
    e, total, _, delta = stats(scores, grad_prob)
    p = e * (1.0 / total)
    ds = (p * (grad_prob - delta)).astype(BF16)
    dq = dot((k * BF16(0.125)).T, ds)
    dq_ref[...] = jnp.concatenate([dq[:64, :REST], dq[64:, REST:]], axis=0).T.astype(BF16)
    sum_ref[0] = dot(ds, q2).astype(BF16)
    sum_ref[1] = dot(p.astype(BF16), g2).astype(BF16)

    @pl.when(step == 3)
    def _():
        store.wait()


def pick_kernel(x_ref, _, b16_ref, b64_ref):
    b16_ref[...] = x_ref[:, :32, :LANES].reshape(256, LANES)
    rows = x_ref[:, :16, :LANES].astype(F32)[:, :8, :].reshape(64, LANES).astype(BF16)
    for a in range(HEADS):
        b64_ref[a] = rows


def products(kv, qg):
    both = dot_tt(kv, pair(qg))
    return both[:, : qg.shape[0]], both[:, qg.shape[0] :]


def spread(row, width, fill):
    lines = []
    for s in range(HEADS):
        piece = row[:, s * width : (s + 1) * width]
        if width < DIL:
            piece = jnp.concatenate([piece, jnp.full((1, DIL - width), fill, F32)], axis=1)
        lines.append(piece)
    return jnp.concatenate(lines, axis=0)


def segment(x_ref, s):
    block = x_ref[4 * s : 4 * s + 4, :DIL, :].reshape(4 * DIL, 2 * LANES)
    return block[:, :LANES], block[:, LANES:]


def second_kernel(x_ref, stat_ref):
    lse, delta = [], []
    for s in range(2):
        scores, grad_prob = products(*segment(x_ref, s))
        got = stats(scores, grad_prob)
        lse.append(got[2])
        delta.append(got[3])
    stat_ref[0] = spread(jnp.concatenate(lse, axis=1), DIL, LOW)
    stat_ref[1] = spread(jnp.concatenate(delta, axis=1), DIL, 0.0)


def third(x_ref, p16_ref):
    block = x_ref[:, :32, :].reshape(256, 2 * LANES)
    return jnp.concatenate([block[:, :LANES], p16_ref[...]], axis=0), block[:, LANES:]


def third_kernel(x_ref, p16_ref, stat_ref):
    got = stats(*products(*third(x_ref, p16_ref)))
    stat_ref[0] = spread(got[2], 32, LOW)
    stat_ref[1] = spread(got[3], 32, 0.0)


def head_kernel(x_ref, second_ref, third_ref, p16_ref, c64_ref, own_ref, dq_ref, part16_ref, part64_ref, stat_ref):
    def grads(kv, qg, scores, grad_prob, lse, delta):
        p = jnp.exp(scores - lse)
        ds = (p * (grad_prob - delta)).astype(BF16)
        dkv = dot(jnp.concatenate([ds, p.astype(BF16)], axis=1), pair(qg))
        dq = dot((kv * BF16(0.125)).T, ds).T
        return dkv, dq

    def collect(table, width):
        return jnp.concatenate([table[s : s + 1, :width] for s in range(HEADS)], axis=1)

    segments = [segment(x_ref, s) for s in range(2)]
    kv16, qg16 = third(x_ref, p16_ref)
    qg64 = x_ref[:, :16, LANES:].astype(F32)[:, :8, :].reshape(64, LANES).astype(BF16)
    kv64 = c64_ref[...].reshape(512, LANES)

    lse1, delta1 = [], []
    for s in range(HEADS):
        rows = x_ref[s, DIL:, :LANES].astype(F32)
        lse1.append(rows[0:1] + rows[1:2] + rows[2:3])
        delta1.append(rows[3:4] + rows[4:5] + rows[5:6])
    lses = [jnp.concatenate(lse1, axis=0)]
    deltas = [jnp.concatenate(delta1, axis=0)]

    lses.append(second_ref[0])
    deltas.append(second_ref[1])
    made16 = products(kv16, qg16)
    lses.append(third_ref[0])
    deltas.append(third_ref[1])
    made64 = products(kv64, qg64)
    got = stats(*made64)
    lses.append(spread(got[2], 8, LOW))
    deltas.append(spread(got[3], 8, 0.0))

    top = functools.reduce(jnp.maximum, lses)
    parts = [jnp.exp(x - top) for x in lses]
    total = sum(parts)
    lse = top + jnp.log(total)
    delta = sum(w * d for w, d in zip(parts, deltas)) / total
    stat_ref[0] = lse
    stat_ref[1] = delta

    for s in range(2):
        row = [jnp.concatenate([t[4 * s + i : 4 * s + i + 1] for i in range(4)], axis=1) for t in (lse, delta)]
        dkv, dq = grads(*segments[s], *products(*segments[s]), *row)
        own_ref[4 * s : 4 * s + 4] = dkv.reshape(4, DIL, LANES)
        dq_ref[4 * s : 4 * s + 4] = dq.reshape(4, DIL, LANES)
    dkv, dq = grads(kv16, qg16, *made16, collect(lse, 32), collect(delta, 32))
    own_ref[:, :32, :] = own_ref[:, :32, :] + dkv[:256].reshape(HEADS, 32, LANES)
    part16_ref[...] = dkv[256:].astype(BF16)
    dq_ref[:, :32, :] = dq_ref[:, :32, :] + dq.reshape(HEADS, 32, LANES)
    dkv, dq = grads(kv64, qg64, *made64, collect(lse, 8), collect(delta, 8))
    part64_ref[...] = dkv.reshape(HEADS, 64, LANES).astype(BF16)
    dq_ref[:, :8, :] = dq_ref[:, :8, :] + dq.reshape(HEADS, 8, LANES)


def gather_kernel(own_ref, dq_ref, got16_ref, got64_ref, out_ref):
    got16 = got16_ref[...].astype(F32).reshape(HEADS, 32, LANES)
    got64 = got64_ref[...].astype(F32)
    got64 = sum(got64[i] for i in range(HEADS)).reshape(HEADS, 8, LANES)
    first = got16[:, :8] + got64
    dkv = own_ref[...]
    dkv = jnp.concatenate([dkv[:, :8] + first, dkv[:, 8:32] + got16[:, 8:], dkv[:, 32:]], axis=1)
    out_ref[:, :DIL, :] = dkv.astype(BF16)
    for s in range(HEADS):
        dq = dq_ref[s]
        out_ref[s, DIL:, :] = jnp.concatenate([dq[:64, :64], dq[64:, :64]], axis=1).astype(BF16)


def rest_kernel(
    st_hbm, far_hbm, in_hbm, kv_hbm, sum_hbm, dq_hbm, wq_hbm, wk_hbm, wv_hbm, send_ref, out_hbm,
    st_ref, in_ref, kv_ref, sum_ref, dq_s, w_s, dk_s, dv_s, pass_s, sems, out_sem,
):
    pairs = [(st_hbm, st_ref.at[pl.ds(0, 4)]), (far_hbm, st_ref.at[pl.ds(4, 4)])]
    pairs += [(in_hbm, in_ref), (kv_hbm, kv_ref), (sum_hbm, sum_ref), (dq_hbm, dq_s)]
    pairs += [(w, w_s.at[i]) for i, w in enumerate((wq_hbm, wk_hbm, wv_hbm))]
    fetches = [pltpu.make_async_copy(a, b, sems.at[i]) for i, (a, b) in enumerate(pairs)]
    for fetch in fetches:
        fetch.start()
    line = lax.rem(lax.axis_index("tm"), 8)
    head = lax.axis_index("head")
    for fetch in fetches[:4]:
        fetch.wait()
    for slab in range(4):
        cols = slice(slab * LANES, (slab + 1) * LANES)
        k, v = kv_ref[0, :, cols], kv_ref[1, :, cols]
        q2, g2 = pair(in_ref[0, :, cols]), pair(in_ref[1, :, cols])
        scores = dot_tt(k, q2)
        grad_prob = dot_tt(v, g2)
        lse, delta = [], []
        for h in range(2):
            at = jnp.bitwise_xor(2 * slab + h, line)
            lse.append(st_ref[at, 0, pl.ds(line, 1), :])
            delta.append(st_ref[at, 1, pl.ds(line, 1), :])
        p = jnp.exp(scores - jnp.concatenate(lse, axis=1))
        ds = (p * (grad_prob - jnp.concatenate(delta, axis=1))).astype(BF16)
        dq = dot((k * BF16(0.125)).T, ds)
        pass_s[0, :DIL, cols] = jnp.concatenate([dq[:64, :DIL], dq[64:, DIL:]], axis=0).T.astype(BF16)
        dk, dv = dot(ds, q2), dot(p.astype(BF16), g2)
        if slab == 0:
            fetches[4].wait()
        dk = (dk + sum_ref[0, :, cols].astype(F32)).astype(BF16)
        dv = (dv + sum_ref[1, :, cols].astype(F32)).astype(BF16)
        pass_s[1, :DIL, cols] = dk[:DIL]
        pass_s[2, :DIL, cols] = dv[:DIL]
        dk_s[:, cols] = dk[DIL:]
        dv_s[:, cols] = dv[DIL:]
    half = REST // 2
    keep = pl.ds(pl.multiple_of(head * half, half), half)
    send = pl.ds(pl.multiple_of((1 - head) * half, half), half)
    fetches[5].wait()
    for i, grad in enumerate((dq_s, dk_s, dv_s)):
        pass_s[i, DIL:, :] = grad[keep, :]
    put = pltpu.make_async_copy(pass_s, out_hbm.at[:, pl.ds(0, PASSED)], out_sem)
    put.start()
    for fetch in fetches[6:]:
        fetch.wait()
    out = dot_tt(dq_s[send, :], w_s[0]) + dot_tt(dk_s[send, :], w_s[1]) + dot_tt(dv_s[send, :], w_s[2])
    send_ref[...] = out.astype(BF16)
    put.wait()


def dil_kernel(perm_ref, got_ref, pass_hbm, w_hbm, keep_ref, send_ref, keep_r, out_s, pass_s, w_s, sems):
    head = lax.axis_index("head")
    fetches = [pltpu.make_async_copy(pass_hbm.at[:, pl.ds(0, PASSED)], pass_s, sems.at[3])]
    fetches += [pltpu.make_async_copy(w_hbm.at[i, pl.ds(0, OWN)], w_s.at[i], sems.at[i]) for i in range(3)]
    for fetch in fetches:
        fetch.start()

    def both(pieces):
        return jnp.concatenate(pieces, axis=1)

    dk = both([got_ref[h, :DIL, :64].astype(F32) for h in range(HEADS)])
    dv = both([got_ref[h, :DIL, 64:].astype(F32) for h in range(HEADS)])
    dq = jnp.concatenate(
        [both([got_ref[h, DIL:, s * 64 : s * 64 + 64].astype(F32) for h in range(HEADS)]) for s in range(2)], axis=0
    )
    perm = perm_ref[...]
    fetches[0].wait()
    grads = [dot(perm, (grad + pass_s[i, :DIL, :].astype(F32)).astype(BF16)).astype(BF16) for i, grad in enumerate((dq, dk, dv))]
    out = None
    for i, rows in enumerate(grads):
        fetches[1 + i].wait()
        part = dot_tt(jnp.concatenate([rows, pass_s[i, DIL:, :]], axis=0), w_s[i])
        out = part if out is None else out + part
    out_s[...] = out[:DIL]
    keep_r[...] = out[DIL:].astype(BF16)
    half = DIL // 2
    keep_ref[...] = out_s[pl.ds(pl.multiple_of(head * half, half), half), :]
    send_ref[...] = out_s[pl.ds(pl.multiple_of((1 - head) * half, half), half), :].astype(BF16)


def last_kernel(perm_ref, keep_d, got_d, keep_r, got_r, out_ref):
    rows = jnp.concatenate(
        [keep_d[...] + got_d[...].astype(F32), keep_r[...].astype(F32) + got_r[...].astype(F32)], axis=0
    ).astype(BF16)
    out_ref[...] = dot(perm_ref[...], rows).astype(BF16)


def params(limit=LARGE):
    return pltpu.CompilerParams(vmem_limit_bytes=limit)


def cost(flops, bytes_accessed, exps):
    return pl.CostEstimate(flops=flops, bytes_accessed=bytes_accessed, transcendentals=exps)


def shape(dims, dtype):
    return jax.ShapeDtypeStruct(dims, dtype)


def slab_spec(rows):
    return pl.BlockSpec((rows, LANES), lambda s: (0, s))


def whole(dims):
    return pl.BlockSpec(dims, lambda s: (0,) * len(dims))


def swap(x, axis, bits):
    return lax.ppermute(x, axis, [(i, i ^ bits) for i in range(lax.axis_size(axis))])


def on_device(queries, keys, values, grad_attn, w_query, w_key, w_value):
    size = lax.axis_size("tm")
    lines = [[a * 8 + j for j in range(8)] for a in range(size // 8)]
    across = [[b * 64 + a * 8 + j for a in range(8)] for b in range(size // 64) for j in range(8)]
    hbm = pl.BlockSpec(memory_space=pltpu.HBM)
    vmem = pl.BlockSpec(memory_space=pltpu.VMEM)
    dil, order = frame_order()
    perm = jnp.asarray(one_hot(order, ROWS), BF16)
    perm_first = jnp.asarray(one_hot(order[:DIL], ROWS), BF16)
    perm_dil = jnp.asarray(one_hot(np.argsort(dil), DIL), BF16)
    f = np.arange(256)
    seat = np.where(f % 4 == 0, f // 4, 64 + f - f // 4 - 1)
    perm_last = jnp.asarray(one_hot(seat, 256), BF16)

    sent = pl.pallas_call(
        pack_kernel,
        in_specs=[hbm] * 5,
        out_specs=hbm,
        out_shape=shape((HEADS, DIL + STAT_ROWS, 256), BF16),
        scratch_shapes=[
            pltpu.VMEM((DIL, ROWS), BF16),
            pltpu.VMEM((4, 4, ROWS, LANES), BF16),
            pltpu.VMEM((HEADS, DIL + STAT_ROWS, 256), BF16),
            pltpu.SemaphoreType.DMA((4, 4)),
            pltpu.SemaphoreType.DMA((4,)),
            pltpu.SemaphoreType.DMA,
        ],
        compiler_params=params(),
        name="pack",
    )(perm_first, queries, keys, values, grad_attn)

    x = lax.all_to_all(sent, "tm", 0, 0, axis_index_groups=lines, tiled=True)

    def stack_spec(planes, rows):
        return pl.BlockSpec((planes, rows, LANES), lambda s: (0, 0, s))

    ins, kv, dq1, sums, weights = pl.pallas_call(
        local_kernel,
        grid=(4,),
        in_specs=[whole((ROWS, ROWS))] + [slab_spec(ROWS)] * 4 + [hbm] * 3,
        out_specs=[
            stack_spec(2, DIL),
            stack_spec(2, ROWS),
            slab_spec(REST),
            stack_spec(2, ROWS),
            hbm,
        ],
        scratch_shapes=[pltpu.VMEM((3, OWN, 512), BF16), pltpu.SemaphoreType.DMA((4,))],
        out_shape=[
            shape((2, DIL, 512), BF16),
            shape((2, ROWS, 512), BF16),
            shape((REST, 512), BF16),
            shape((2, ROWS, 512), BF16),
            shape((3, TALL, 512), BF16),
        ],
        compiler_params=params(),
        cost_estimate=cost(12_000_000_000, 5_000_000, 1_600_000),
        name="local",
    )(perm, queries, keys, values, grad_attn, w_query, w_key, w_value)

    mine16, mine64 = pl.pallas_call(
        pick_kernel,
        in_specs=[vmem, hbm],
        out_shape=[shape((256, LANES), BF16), shape((8, 64, LANES), BF16)],
        compiler_params=params(32 * MIB),
        name="pick",
    )(x, weights)
    p16 = swap(mine16, "tm", 8)
    c64 = lax.all_to_all(mine64, "tm", 0, 0, axis_index_groups=across, tiled=True)
    second = pl.pallas_call(
        second_kernel,
        out_shape=shape((2, HEADS, DIL), F32),
        compiler_params=params(24 * MIB),
        cost_estimate=cost(2_000_000_000, 4_000_000, 500_000),
        name="second",
    )(x)
    third_stats = pl.pallas_call(
        third_kernel,
        out_shape=shape((2, HEADS, DIL), F32),
        compiler_params=params(24 * MIB),
        cost_estimate=cost(1_000_000_000, 2_000_000, 130_000),
        name="third",
    )(x, p16)
    own, dq_own, part16, part64, stat = pl.pallas_call(
        head_kernel,
        out_shape=[
            shape((HEADS, DIL, LANES), F32),
            shape((HEADS, DIL, LANES), F32),
            shape((256, LANES), BF16),
            shape((8, 64, LANES), BF16),
            shape((2, HEADS, DIL), F32),
        ],
        compiler_params=params(24 * MIB),
        name="heads",
    )(x, second, third_stats, p16, c64)

    st = stat[None]
    for bit in (1, 2):
        st = jnp.concatenate([st, swap(st, "tm", bit)], axis=0)
    st_far = swap(st, "tm", 4)
    got16 = swap(part16, "tm", 8)
    got64 = lax.all_to_all(part64, "tm", 0, 0, axis_index_groups=across, tiled=True)
    back = pl.pallas_call(
        gather_kernel,
        out_shape=shape((HEADS, DIL + 64, LANES), BF16),
        compiler_params=params(8 * MIB),
        name="gather",
    )(own, dq_own, got16, got64)
    got = lax.all_to_all(back, "tm", 0, 0, axis_index_groups=lines, tiled=True)

    half = REST // 2
    send_r, passed = pl.pallas_call(
        rest_kernel,
        in_specs=[hbm] * 9,
        out_specs=[vmem, hbm],
        out_shape=[shape((half, 1024), BF16), shape((3, TALL, 512), BF16)],
        scratch_shapes=[
            pltpu.VMEM((8, 2, HEADS, DIL), F32),
            pltpu.VMEM((2, DIL, 512), BF16),
            pltpu.VMEM((2, ROWS, 512), BF16),
            pltpu.VMEM((2, ROWS, 512), BF16),
            pltpu.VMEM((REST, 512), BF16),
            pltpu.VMEM((3, OWN, 512), BF16),
            pltpu.VMEM((REST, 512), BF16),
            pltpu.VMEM((REST, 512), BF16),
            pltpu.VMEM((3, PASSED, 512), BF16),
            pltpu.SemaphoreType.DMA((9,)),
            pltpu.SemaphoreType.DMA,
        ],
        compiler_params=params(),
        cost_estimate=cost(5_000_000_000, 9_000_000, 600_000),
        name="rest",
    )(st, st_far, ins, kv, sums, dq1, w_query, w_key, w_value)
    got_r = swap(send_r, "head", 1)

    keep_d, send_d, keep_r = pl.pallas_call(
        dil_kernel,
        in_specs=[vmem] * 2 + [hbm] * 2,
        out_shape=[shape((DIL // 2, 1024), F32), shape((DIL // 2, 1024), BF16), shape((half, 1024), BF16)],
        scratch_shapes=[
            pltpu.VMEM((DIL, 1024), F32),
            pltpu.VMEM((3, PASSED, 512), BF16),
            pltpu.VMEM((3, OWN, 512), BF16),
            pltpu.SemaphoreType.DMA((4,)),
        ],
        compiler_params=params(24 * MIB),
        name="dil",
    )(perm_dil, got, passed, weights)
    got_d = swap(send_d, "head", 1)
    return pl.pallas_call(
        last_kernel,
        out_shape=shape((256, 1024), BF16),
        compiler_params=params(8 * MIB),
        name="last",
    )(perm_last, keep_d, got_d, keep_r, got_r)


def solution(mesh):
    return jax.shard_map(
        on_device,
        mesh=mesh,
        in_specs=(
            P("tm", "head"),
            P("tm", "head"),
            P("tm", "head"),
            P("tm", "head"),
            P(None, "head"),
            P(None, "head"),
            P(None, "head"),
        ),
        out_specs=P(("tm", "head"), None),
        check_vma=False,
    )
```
